32 devices in a mesh: dp: 8 (over z, x), tensor: 4 (over y, core).
Axes of the slice: x: 2, y: 2, z: 4, core: 2. Of those that a mesh axis runs over, the one named last changes fastest.
Arguments:
- block_input: bfloat16 [8, 2048, 1024], P('dp', 'tensor'), may hold values from -6 to 6
- segment_ids: int32 [8, 2048], P('dp', 'tensor'), may hold values from 0 to 3, as said below
- w_qkv: bfloat16 [3, 1024, 1024], P(None, None, 'tensor'), may hold values from -0.1875 to 0.1875
- w_out: bfloat16 [1024, 1024], P('tensor'), may hold values from -0.75 to 0.75
- w_up: bfloat16 [1024, 4096], P(None, 'tensor'), may hold values from -0.1875 to 0.1875
- w_down: bfloat16 [4096, 1024], P('tensor'), may hold values from -0.09375 to 0.09375
- ln1_gain: float32 [1024], replicated, may hold values from 0.5 to 1.5
- ln1_bias: float32 [1024], replicated, may hold values from -1 to 1
- ln2_gain: float32 [1024], replicated, may hold values from 0.5 to 1.5
- ln2_bias: float32 [1024], replicated, may hold values from -1 to 1
- out_bias: float32 [1024], replicated, may hold values from -1 to 1
- down_bias: float32 [1024], replicated, may hold values from -1 to 1
- cotangent: bfloat16 [8, 2048, 1024], P('dp', 'tensor'), may hold values from -6 to 6
Outputs:
- block_output: bfloat16 [8, 2048, 1024], P('dp', 'tensor')
- x_grad: float32 [8, 2048, 1024], P('dp', 'tensor')
- w_qkv_grad: float32 [3, 1024, 1024], P(None, 'dp', 'tensor')
- w_out_grad: float32 [1024, 1024], P('tensor', 'dp')
- w_up_grad: float32 [1024, 4096], P('dp', 'tensor')
- w_down_grad: float32 [4096, 1024], P('tensor', 'dp')
- ln1_gain_grad: float32 [1024], P(('dp', 'tensor'))
- ln1_bias_grad: float32 [1024], P(('dp', 'tensor'))
- ln2_gain_grad: float32 [1024], P(('dp', 'tensor'))
- ln2_bias_grad: float32 [1024], P(('dp', 'tensor'))
- out_bias_grad: float32 [1024], P(('dp', 'tensor'))
- down_bias_grad: float32 [1024], P(('dp', 'tensor'))
The draws below stay inside these ranges and needn't reach their ends.
Inputs may be any that keep to these rules, and one draw needn't show every extreme that they name: `segment_ids`: in every row the ids run 1, 2, 3 in order and then 0 for padding to the row's end; article 1 holds the first 1 to 256 slots, article 2 ends in the last eighth of the row, and every row has at least one padding slot.
All inputs are finite; a program needn't handle non-finite values.
Results may differ from the reference program's by a relative error of at most 0.018.
Values may be sent and summed in bfloat16 or wider, within the bound.
No kernel may reach another device: no remote copies, remote signals or barrier semaphores. Data moves between devices by JAX's collectives and lax.ppermute only.
A program may use at most 192 MiB of HBM per device.

```python
import jax
import jax.numpy as jnp
from jax import lax

D = 1024
H = 8
HD = 128
FF = 4096
LEN = 2048
ROWS = 8
QB = 512


def draw_segment_ids(key, part):
    key = jax.random.fold_in(key, 7)
    first_key, second_key, third_key = jax.random.split(key, 3)
    first_cut = jax.random.randint(first_key, (ROWS, 1), 1, LEN // 8 + 1)
    second_cut = jax.random.randint(second_key, (ROWS, 1), LEN - LEN // 8, LEN - LEN // 32)
    pad_start = jax.random.randint(third_key, (ROWS, 1), second_cut + 1, LEN)
    places = jnp.arange(LEN, dtype=jnp.int32)[None, :]
    return jnp.where(places < first_cut, 1, jnp.where(places < second_cut, 2, jnp.where(places < pad_start, 3, 0))).astype(jnp.int32)


def shard_levels(own_key, shape, pieces, smallest, high):
    factor_of, own = 1.0, jax.random.fold_in(own_key, 6)
    for dim, blocks in pieces:
        heights = jnp.exp(jax.random.uniform(jax.random.fold_in(own, dim), (blocks,), jnp.float32, smallest / len(pieces), high / len(pieces)))
        factor_of = factor_of * jnp.repeat(heights, shape[dim] // blocks).reshape([-1 if axis == dim else 1 for axis in range(len(shape))])
    return factor_of


def normal_values(rng, shape, deviation, limit, cuts=(), held_as=jnp.bfloat16):
    values = jax.random.normal(rng, shape, jnp.float32) * deviation
    if len(cuts) > 0:
        values = shard_levels(rng, shape, cuts, -0.22, 0.18) * values
    return jnp.clip(values, min=-limit, max=limit).astype(held_as)


def setup_inputs(seed: int = 0) -> dict:
    key_of = jax.random.split(jax.random.key(seed), 14)
    return {
        "block_input": normal_values(key_of[0], (ROWS, LEN, D), 1.0, 6.0, ((0, 8), (1, 4))),
        "segment_ids": draw_segment_ids(jax.random.fold_in(key_of[13], 71), 0),
        "w_qkv": normal_values(key_of[2], (3, D, H * HD), D ** -0.5, 0.1875, ((2, 4),)),
        "w_out": normal_values(key_of[3], (H * HD, D), (H * HD // 16) ** -0.5, 0.75, ((0, 4),)),
        "w_up": normal_values(key_of[4], (D, FF), D ** -0.5, 0.1875, ((1, 4),)),
        "w_down": normal_values(key_of[5], (FF, D), FF ** -0.5, 0.09375, ((0, 4),)),
        "ln1_gain": jnp.clip(1.0 + 0.1 * jax.random.normal(key_of[6], (D,), jnp.float32), 0.5, 1.5),
        "ln1_bias": normal_values(key_of[7], (D,), 0.2, 1.0, (), jnp.float32),
        "ln2_gain": jnp.clip(1.0 + 0.1 * jax.random.normal(key_of[8], (D,), jnp.float32), 0.5, 1.5),
        "ln2_bias": normal_values(key_of[9], (D,), 0.2, 1.0, (), jnp.float32),
        "out_bias": normal_values(key_of[10], (D,), 0.2, 1.0, (), jnp.float32),
        "down_bias": normal_values(key_of[11], (D,), 0.2, 1.0, (), jnp.float32),
        "cotangent": normal_values(key_of[12], (ROWS, LEN, D), 1.0, 6.0, ((0, 8), (1, 4))),
    }


@jax.custom_vjp
def low(v):
    return lax.optimization_barrier(v.astype(jnp.bfloat16)).astype(jnp.float32)

@jax.custom_vjp
def low_back(v):
    return v

def low_keep(v):
    return (low(v), None)

def low_pass(kept, grad):
    return (grad,)

def back_keep(v):
    return (v, None)

def back_low(kept, grad):
    return (low(grad),)
low.defvjp(low_keep, low_pass)
low_back.defvjp(back_keep, back_low)
EPS = 1e-05
NEG = -1e+30
TOP = lax.Precision.HIGHEST

def layer_norm(values, gain, shift):
    center = values - lax.optimization_barrier(jnp.mean(values, -1, keepdims=True))
    spread = lax.optimization_barrier(jnp.mean(center * center, -1, keepdims=True))
    return center * lax.rsqrt(spread + EPS) * gain + shift

def block_scores(queries, keys, seg_query, seg_key, start, slopes):
    count = queries.shape[0]
    scale = queries.shape[-1] ** (-0.5)
    raw = jnp.einsum('qhd,khd->hqk', queries, keys, precision=TOP) * scale
    query_place = start + jnp.arange(count, dtype=jnp.int32)
    key_place = jnp.arange(keys.shape[0], dtype=jnp.int32)
    distance = (query_place[:, None] - key_place[None, :]).astype(jnp.float32)
    allowed = (seg_query[:, None] == seg_key[None, :]) & (key_place[None, :] <= query_place[:, None])
    return jnp.where(allowed[None], raw - slopes[:, None, None] * distance[None], NEG)

def row_forward(params, x_row, seg_row):
    w_qkv, w_out, w_up, w_down, gain_one, shift_one, gain_two, shift_two, bias_out, bias_down = params
    normed = low(layer_norm(x_row, gain_one, shift_one))
    projected = jnp.einsum('ld,cde->cle', normed, w_qkv, precision=TOP)
    projected = low(low_back(projected))
    shaped = projected.reshape(3, LEN, H, HD)
    queries, keys, values = (shaped[0], shaped[1], shaped[2])
    slopes = jnp.exp2(-8.0 * (1 + jnp.arange(H, dtype=jnp.int32)).astype(jnp.float32) / H)
    blocks = LEN // QB

    def attend(index):
        start = (index * QB).astype(jnp.int32)
        query_block = lax.dynamic_slice_in_dim(queries, start, QB, 0)
        seg_query = lax.dynamic_slice_in_dim(seg_row, start, QB, 0)
        scores = low_back(block_scores(query_block, keys, seg_query, seg_row, start, slopes))
        row_max = lax.optimization_barrier(jnp.max(scores, -1, keepdims=True))
        exponent = jnp.exp(scores - row_max)
        probs = exponent / lax.optimization_barrier(jnp.sum(exponent, -1, keepdims=True))
        return jnp.einsum('hqk,khd->qhd', low(probs), values, precision=TOP)
    mixed = lax.map(jax.checkpoint(attend), jnp.arange(blocks, dtype=jnp.int32)).reshape(LEN, H * HD)
    mixed = low(low_back(mixed))
    attn = low_back(jnp.dot(mixed, w_out, precision=TOP)) + bias_out
    resid = x_row + attn
    normed_two = low(layer_norm(resid, gain_two, shift_two))
    pre_act = low_back(jnp.dot(normed_two, w_up, precision=TOP))
    activated = low(jax.nn.gelu(pre_act, approximate=True))
    ffn = low_back(jnp.dot(activated, w_down, precision=TOP)) + bias_down
    valid = (seg_row != 0).astype(jnp.float32)
    return valid[:, None] * (resid + ffn)

def reference(block_input, segment_ids, w_qkv, w_out, w_up, w_down, ln1_gain, ln1_bias, ln2_gain, ln2_bias, out_bias, down_bias, cotangent):
    params = (w_qkv.astype(jnp.float32), w_out.astype(jnp.float32), w_up.astype(jnp.float32), w_down.astype(jnp.float32), ln1_gain.astype(jnp.float32), ln1_bias.astype(jnp.float32), ln2_gain.astype(jnp.float32), ln2_bias.astype(jnp.float32), out_bias.astype(jnp.float32), down_bias.astype(jnp.float32))

    def step(carry, item):
        x_row, seg_row, grad_row = item

        def forward(weights, inputs):
            return row_forward(weights, inputs, seg_row)
        output, backward = jax.vjp(forward, params, x_row)
        grads, input_grad = backward(grad_row)
        carry = jax.tree.map(jnp.add, carry, grads)
        return (carry, (output.astype(jnp.bfloat16), input_grad))
    zeros = jax.tree.map(jnp.zeros_like, params)
    totals, outputs = lax.scan(step, zeros, (block_input.astype(jnp.float32), segment_ids, cotangent.astype(jnp.float32)))
    return (outputs[0], outputs[1], totals[0], totals[1], totals[2], totals[3], totals[4], totals[5], totals[6], totals[7], totals[8], totals[9])
```

```python
import functools

import jax
import jax.numpy as jnp
from jax import lax
from jax.experimental import pallas as pl
from jax.experimental.pallas import tpu as pltpu
from jax.sharding import PartitionSpec as P

H = 8
HD = 128
EPS = 1e-05
NEG = -1e30
LOG2E = 1.4426950408889634
BF = jnp.bfloat16
F32 = jnp.float32
NN = (((1,), (0,)), ((), ()))
NT = (((1,), (1,)), ((), ()))
TN = (((0,), (0,)), ((), ()))
VMEM = pl.BlockSpec(memory_space=pltpu.VMEM)
SMEM = pl.BlockSpec(memory_space=pltpu.SMEM)


def dot(a, b, dims=NN):
    return lax.dot_general(a, b, dims, preferred_element_type=F32)


def split3(v):
    hi = v.astype(BF)
    rest = v - hi.astype(F32)
    mid = rest.astype(BF)
    return hi, mid, (rest - mid.astype(F32)).astype(BF)


def attn_fwd_kernel(size, block, heads, t_ref, qkv_ref, qx_ref, kx_ref, o_ref, qx2_ref, qa, ka, va):
    t = t_ref[0]
    pieces = 4
    width = heads * HD
    lane = lax.broadcasted_iota(jnp.int32, (size, HD), 1)
    ones = jnp.where(lane == 0, 1.0, 0.0).astype(BF)
    for r in range(pieces):
        to = pl.ds(pl.multiple_of((t ^ r) * size, size), size)
        src = slice(r * size, (r + 1) * size)
        for h in range(heads):
            qa[h, to, :HD] = qkv_ref[src, h * HD : (h + 1) * HD]
            ka[h, to, :HD] = qkv_ref[src, width + h * HD : width + (h + 1) * HD]
            va[h, to, :HD] = qkv_ref[src, 2 * width + h * HD : 2 * width + (h + 1) * HD]
            va[h, to, HD:] = ones
            qa[h, to, HD:] = qx_ref[src, :]
            ka[h, to, HD:] = kx_ref[h, src, :]
    row = lax.broadcasted_iota(jnp.int32, (block, block), 0)
    col = lax.broadcasted_iota(jnp.int32, (block, block), 1)
    keep = col <= row
    lane = lax.broadcasted_iota(jnp.int32, (block, HD), 1)
    per = size // block
    for i in range(pieces * per):
        start = i * block
        end = start + block
        at = pl.ds(pl.multiple_of(((i // per) ^ t) * size + (i % per) * block, block), block)
        for h in range(heads):
            q = qa[h, start:end, :]
            near = jnp.where(keep, dot(q, ka[h, start:end, :], NT), NEG)
            top = jnp.max(near, -1, keepdims=True)
            if i:
                far = dot(q, ka[h, :start, :], NT)
                top = jnp.maximum(top, jnp.max(far, -1, keepdims=True))
            out = dot(jnp.exp2(near - top).astype(BF), va[h, start:end, :])
            if i:
                out = out + dot(jnp.exp2(far - top).astype(BF), va[h, :start, :])
            total = out[:, HD : HD + 1]
            o_ref[at, h * HD : (h + 1) * HD] = (out[:, :HD] / total).astype(BF)
            hi, mid, lo = split3(-(top + jnp.log2(total)))
            extra = qa[h, start:end, HD:]
            extra = jnp.where(lane == 7, hi, jnp.where(lane == 8, mid, jnp.where(lane == 9, lo, extra)))
            qx2_ref[h, at, :] = extra


def attn_fwd(t, qkv, qx, kx, block=512):
    length = qkv.shape[0]
    width = qkv.shape[1] // 3
    heads = width // HD
    return pl.pallas_call(
        functools.partial(attn_fwd_kernel, length // 4, block, heads),
        out_shape=(
            jax.ShapeDtypeStruct((length, width), BF),
            jax.ShapeDtypeStruct((heads, length, HD), BF),
        ),
        in_specs=[SMEM, VMEM, VMEM, VMEM],
        out_specs=(VMEM, VMEM),
        scratch_shapes=[pltpu.VMEM((heads, length, 2 * HD), BF)] * 3,
        name="attn_fwd",
        cost_estimate=pl.CostEstimate(flops=8 * 10**9, bytes_accessed=16 * 10**6, transcendentals=0),
        compiler_params=pltpu.CompilerParams(vmem_limit_bytes=56 * 2**20),
    )(t, qkv, qx, kx)


def attn_bwd_kernel(size, block, heads, t_ref, qkv_ref, do_ref, o_ref, qx_ref, kx_ref, g_ref, qa, ka, da, va, dqt):
    t = t_ref[0]
    pieces = 4
    length = pieces * size
    width = heads * HD
    lane = lax.broadcasted_iota(jnp.int32, (size, HD), 1)
    ones = jnp.where(lane < 3, 1.0, 0.0).astype(BF)
    for r in range(pieces):
        to = pl.ds(pl.multiple_of((t ^ r) * size, size), size)
        src = slice(r * size, (r + 1) * size)
        for h in range(heads):
            sl = slice(h * HD, (h + 1) * HD)
            qa[h, to, :HD] = qkv_ref[src, sl]
            qa[h, to, HD:] = qx_ref[h, src, :]
            ka[h, to, :HD] = qkv_ref[src, width + h * HD : width + (h + 1) * HD]
            ka[h, to, HD:] = kx_ref[h, src, :]
            va[h, to, :HD] = qkv_ref[src, 2 * width + h * HD : 2 * width + (h + 1) * HD]
            va[h, to, HD:] = ones
            do = do_ref[src, sl]
            delta = jnp.sum(do.astype(F32) * o_ref[src, sl].astype(F32), -1, keepdims=True)
            hi, mid, lo = split3(-delta)
            da[h, to, :HD] = do
            da[h, to, HD:] = jnp.where(lane == 0, hi, jnp.where(lane == 1, mid, jnp.where(lane == 2, lo, BF(0))))
    row = lax.broadcasted_iota(jnp.int32, (block, block), 0)
    col = lax.broadcasted_iota(jnp.int32, (block, block), 1)
    keep = row <= col
    per = size // block
    for j in range(pieces * per):
        start = j * block
        end = start + block
        at = pl.ds(pl.multiple_of(((j // per) ^ t) * size + (j % per) * block, block), block)
        for h in range(heads):
            k = ka[h, start:end, :]
            v = va[h, start:end, :]

            def part(a, b, masked):
                s = dot(k, qa[h, a:b, :], NT)
                if masked:
                    s = jnp.where(keep, s, NEG)
                p = jnp.exp2(s)
                ds = (p * dot(v, da[h, a:b, :], NT)).astype(BF)
                dv = dot(p.astype(BF), da[h, a:b, :HD])
                dk = dot(ds, qa[h, a:b, :HD])
                dq = dot(k[:, :HD], ds, TN)
                if j:
                    dqt[h, :, a:b] += dq
                else:
                    dqt[h, :, a:b] = dq
                return dk, dv

            dk, dv = part(start, end, True)
            if end < length:
                dk_far, dv_far = part(end, length, False)
                dk, dv = dk + dk_far, dv + dv_far
            g_ref[at, h * HD : (h + 1) * HD] = (dqt[h, :, start:end].T * HD**-0.5).astype(BF)
            g_ref[at, width + h * HD : width + (h + 1) * HD] = (dk * (1.0 / LOG2E)).astype(BF)
            g_ref[at, 2 * width + h * HD : 2 * width + (h + 1) * HD] = dv.astype(BF)


def attn_bwd(t, qkv, do, o, qx, kx, block=512):
    length = qkv.shape[0]
    width = qkv.shape[1] // 3
    heads = width // HD
    return pl.pallas_call(
        functools.partial(attn_bwd_kernel, length // 4, block, heads),
        out_shape=jax.ShapeDtypeStruct(qkv.shape, BF),
        in_specs=[SMEM] + [VMEM] * 5,
        out_specs=VMEM,
        scratch_shapes=[pltpu.VMEM((heads, length, 2 * HD), BF)] * 4 + [pltpu.VMEM((heads, HD, length), F32)],
        name="attn_bwd",
        cost_estimate=pl.CostEstimate(flops=14 * 10**9, bytes_accessed=24 * 10**6, transcendentals=0),
        compiler_params=pltpu.CompilerParams(vmem_limit_bytes=56 * 2**20),
    )(t, qkv, do, o, qx, kx)


def position_columns(t, segments, heads):
    length = segments.shape[0]
    size = length // 4
    lane = jnp.arange(HD, dtype=jnp.int32)[None, :]
    hot = (segments[:, None] == lane - 3) & (lane >= 3) & (lane < 7)
    qx = jnp.where((lane < 3) | hot, 1.0, 0.0).astype(BF)
    index = jnp.arange(length, dtype=jnp.int32)
    place = ((index // size) ^ t) * size + index % size
    slopes = jnp.exp2(-8.0 * (t * heads + 1 + jnp.arange(heads, dtype=jnp.int32)).astype(F32) / H) * LOG2E
    bias = slopes[:, None, None] * place.astype(F32)[None, :, None]
    hi = lax.reduce_precision(bias, 8, 7)
    mid = lax.reduce_precision(bias - hi, 8, 7)
    lo = bias - hi - mid
    base = jnp.where(
        (lane >= 3) & (lane < 7), jnp.where(hot, 0.0, NEG), jnp.where((lane >= 7) & (lane < 10), 1.0, 0.0)
    )[None]
    kx = jnp.where(lane == 0, hi, jnp.where(lane == 1, mid, jnp.where(lane == 2, lo, base))).astype(BF)
    return qx, kx


def to_core(x):
    return lax.ppermute(x, "tensor", [(i, i ^ 1) for i in range(4)])


def to_chip(x):
    return lax.ppermute(x, "tensor", [(i, i ^ 2) for i in range(4)])


def to_diag(x):
    return lax.ppermute(x, "tensor", [(i, i ^ 3) for i in range(4)])


def gather(x):
    far = to_chip(x)
    return [x, to_core(x), far, to_core(far)]


def scatter_sum(parts):
    chip = (parts[2].astype(F32) + to_core(parts[3]).astype(F32)).astype(BF)
    return parts[0].astype(F32) + to_core(parts[1]).astype(F32) + to_chip(chip).astype(F32)


def dp_steps(size, first):
    bits = list(range(size.bit_length() - 1))
    return bits[first:] + bits[:first]


def dp_reduce(x, size, index, first):
    bits = size.bit_length() - 1
    shape = x.shape[1:]
    x = x.reshape((2,) * bits + shape)
    axes = list(range(bits - 1, -1, -1))
    for bit in dp_steps(size, first):
        axis = axes.index(bit)
        mine = (index >> bit) & 1
        send = lax.dynamic_index_in_dim(x, 1 - mine, axis, keepdims=False).astype(BF)
        keep = lax.dynamic_index_in_dim(x, mine, axis, keepdims=False)
        got = lax.ppermute(send, "dp", [(i, i ^ (1 << bit)) for i in range(size)])
        x = keep.astype(F32) + got.astype(F32)
        axes.remove(bit)
    return x


def layer_norm(values, gain, shift):
    center = values - jnp.mean(values, -1, keepdims=True)
    spread = jnp.mean(center * center, -1, keepdims=True)
    return center * lax.rsqrt(spread + EPS) * gain + shift


def normalized(values):
    center = values - jnp.mean(values, -1, keepdims=True)
    inverse = lax.rsqrt(jnp.mean(center * center, -1, keepdims=True) + EPS)
    return center * inverse, inverse


def norm_back(grad, gain, hat, inverse):
    e = grad * gain
    return (e - jnp.mean(e, -1, keepdims=True) - hat * jnp.mean(e * hat, -1, keepdims=True)) * inverse


def gelu_smooth(values):
    return jax.nn.gelu(values, approximate=True)


def local(dp, block_input, segment_ids, w_qkv, w_out, w_up, w_down, ln1_gain, ln1_bias, ln2_gain, ln2_bias, out_bias, down_bias, cotangent):
    size, width = block_input.shape[1:]
    length = 4 * size
    local_width = w_qkv.shape[2]
    heads = local_width // HD
    t = lax.axis_index("tensor")
    d = lax.axis_index("dp")
    t_arg = t[None].astype(jnp.int32)
    x = block_input[0].astype(F32)
    seg = segment_ids[0]
    hat_one, inverse_one = normalized(x)
    n1 = (hat_one * ln1_gain + ln1_bias).astype(BF)
    segments = jnp.concatenate(gather(seg))
    qx, kx = position_columns(t, segments, heads)
    n1_all = jnp.concatenate(gather(n1))
    valid = (seg != 0).astype(F32)[:, None]
    grad_out = valid * cotangent[0].astype(F32)
    dffn_own = grad_out.astype(BF)
    wo = gather(w_out)
    dffn = jnp.concatenate(gather(dffn_own))

    q_scale = HD**-0.5 * LOG2E
    projected = [dot(n1_all, w_qkv[c]) for c in range(3)]
    qkv = jnp.concatenate([projected[0] * q_scale, projected[1], projected[2]], -1).astype(BF)
    mixed, qx2 = attn_fwd(t_arg, qkv, qx, kx)
    mixed_sent = mixed.reshape(4, size, local_width)
    mixed_own = jnp.concatenate(
        [mixed_sent[0], to_core(mixed_sent[1]), to_chip(mixed_sent[2]), to_diag(mixed_sent[3])], -1
    )
    wo_all = jnp.concatenate(wo)
    resid = x + dot(mixed_own, wo_all) + out_bias
    hat_two, inverse_two = normalized(resid)
    n2 = jnp.concatenate(gather((hat_two * ln2_gain + ln2_bias).astype(BF)))
    pre = dot(n2, w_up)
    activated, gelu_back = jax.vjp(gelu_smooth, pre)
    act = activated.astype(BF)
    dact = dot(dffn, w_down, NT)
    dpre = gelu_back(dact)[0].astype(BF)
    dn2_parts = dot(dpre, w_up, NT).astype(BF).reshape(4, size, width)
    dn2 = scatter_sum(dn2_parts)
    ffn_parts = dot(act, w_down).astype(BF).reshape(4, size, width)
    up_grad = dot(n2, dpre, TN)
    down_grad = dot(act, dffn, TN)

    dresid = grad_out + norm_back(dn2, ln2_gain, hat_two, inverse_two)
    dattn = dresid.astype(BF)
    dmixed_own = dot(dattn, wo_all, NT).astype(BF).reshape(size, 4, local_width)
    dmixed = jnp.concatenate(
        [dmixed_own[:, 0], to_core(dmixed_own[:, 1]), to_chip(dmixed_own[:, 2]), to_diag(dmixed_own[:, 3])]
    )
    out_grad = dot(mixed_own, dattn, TN).astype(BF).reshape(4, local_width, width)
    ffn = scatter_sum(ffn_parts)
    output = (valid * (resid + ffn + down_bias)).astype(BF)
    dqkv = attn_bwd(t_arg, qkv, dmixed, mixed, qx2, kx)
    w_flat = jnp.concatenate([w_qkv[0], w_qkv[1], w_qkv[2]], -1)
    dn1 = scatter_sum(dot(dqkv, w_flat, NT).astype(BF).reshape(4, size, width))
    qkv_grad = dot(n1_all, dqkv, TN)
    x_grad = dresid + norm_back(dn1, ln1_gain, hat_one, inverse_one)

    out_sum = scatter_sum(out_grad)
    up_rows = width // dp
    qkv_sum = dp_reduce(qkv_grad.reshape(dp, up_rows, 3 * local_width), dp, d, 0)
    qkv_final = qkv_sum.reshape(up_rows, 3, local_width).transpose(1, 0, 2)
    up_final = dp_reduce(up_grad.reshape(dp, up_rows, w_up.shape[1]), dp, d, 0)
    down_final = dp_reduce(down_grad.reshape(w_down.shape[0], dp, up_rows).transpose(1, 0, 2), dp, d, 1)
    out_final = dp_reduce(out_sum.reshape(local_width, dp, up_rows).transpose(1, 0, 2), dp, d, 1)
    vectors = jnp.stack(
        [
            jnp.sum(dn1 * hat_one, 0),
            jnp.sum(dn1, 0),
            jnp.sum(dn2 * hat_two, 0),
            jnp.sum(dn2, 0),
            jnp.sum(dresid, 0),
            jnp.sum(grad_out, 0),
        ]
    )
    bits = dp.bit_length() - 1
    chunk = width // dp // 4
    vectors = vectors.reshape(6, dp, 4, chunk).transpose(1, 2, 0, 3)
    for step in range(2):
        bit = 1 - step
        mine = (t >> bit) & 1
        view = vectors.reshape((dp,) + (2,) * (2 - step) + (6, chunk))
        send = lax.dynamic_index_in_dim(view, 1 - mine, 1, keepdims=False)
        vectors = lax.dynamic_index_in_dim(view, mine, 1, keepdims=False) + lax.ppermute(
            send, "tensor", [(i, i ^ (1 << bit)) for i in range(4)]
        )
    vectors = vectors.reshape((2,) * bits + (6, chunk))
    for bit in range(bits - 1, -1, -1):
        mine = (d >> bit) & 1
        send = lax.dynamic_index_in_dim(vectors, 1 - mine, 0, keepdims=False)
        vectors = lax.dynamic_index_in_dim(vectors, mine, 0, keepdims=False) + lax.ppermute(
            send, "dp", [(i, i ^ (1 << bit)) for i in range(dp)]
        )
    return (
        output[None],
        x_grad[None],
        qkv_final,
        out_final.reshape(local_width, up_rows),
        up_final,
        down_final.reshape(w_down.shape[0], up_rows),
        vectors[0],
        vectors[1],
        vectors[2],
        vectors[3],
        vectors[4],
        vectors[5],
    )


def solution(mesh):
    row = P("dp", "tensor", None)
    in_specs = (
        row,
        P("dp", "tensor"),
        P(None, None, "tensor"),
        P("tensor", None),
        P(None, "tensor"),
        P("tensor", None),
        P(),
        P(),
        P(),
        P(),
        P(),
        P(),
        row,
    )
    vector = P(("dp", "tensor"))
    out_specs = (row, row, P(None, "dp", "tensor"), P("tensor", "dp"), P("dp", "tensor"), P("tensor", "dp")) + (vector,) * 6
    run = functools.partial(local, mesh.shape["dp"])
    return jax.shard_map(run, mesh=mesh, in_specs=in_specs, out_specs=out_specs, check_vma=False)
```

```python
import functools

import jax
import jax.numpy as jnp
from jax import lax
from jax.experimental import pallas as pl
from jax.experimental.pallas import tpu as pltpu
from jax.sharding import PartitionSpec as P

H = 8
HD = 128
EPS = 1e-05
NEG = -1e30
LOG2E = 1.4426950408889634
BF = jnp.bfloat16
F32 = jnp.float32
NN = (((1,), (0,)), ((), ()))
NT = (((1,), (1,)), ((), ()))
TN = (((0,), (0,)), ((), ()))
VMEM = pl.BlockSpec(memory_space=pltpu.VMEM)
SMEM = pl.BlockSpec(memory_space=pltpu.SMEM)


def dot(a, b, dims=NN):
    return lax.dot_general(a, b, dims, preferred_element_type=F32)


def call(name, body, outs, args, limit=12, scratch=(), scalars=0, blocks=None):
    in_specs, out_specs, grid = blocks or ([SMEM] * scalars + [VMEM] * (len(args) - scalars), (VMEM,) * len(outs), ())
    return pl.pallas_call(
        body,
        out_shape=tuple(outs),
        grid=grid,
        in_specs=in_specs,
        out_specs=out_specs,
        scratch_shapes=list(scratch),
        name=name,
        cost_estimate=pl.CostEstimate(flops=1, bytes_accessed=1, transcendentals=0),
        compiler_params=pltpu.CompilerParams(vmem_limit_bytes=limit * 2**20),
    )(*args)


def arr(shape, dtype=BF):
    return jax.ShapeDtypeStruct(shape, dtype)


def split3(v):
    hi = v.astype(BF)
    rest = v - hi.astype(F32)
    mid = rest.astype(BF)
    return hi, mid, (rest - mid.astype(F32)).astype(BF)


def standardized(values):
    center = values - jnp.mean(values, -1, keepdims=True)
    inverse = lax.rsqrt(jnp.mean(center * center, -1, keepdims=True) + EPS)
    return center * inverse, inverse


def norm_back(grad, gain, hat, inverse):
    e = grad * gain
    return (e - jnp.mean(e, -1, keepdims=True) - hat * jnp.mean(e * hat, -1, keepdims=True)) * inverse


def bits_of(index, place, value):
    return pl.multiple_of((index ^ place) * value, value)


class Order:
    def __init__(self):
        self.last = ()

    def __call__(self, name, body, outs, args, limit=12, scratch=(), scalars=0, blocks=None):
        args = list(args)
        if self.last:
            args[scalars] = after(args[scalars], *self.last)
        got = call(name, body, outs, args, limit, scratch, scalars, blocks)
        self.last = (got[-1],)
        return got

    def then(self, x):
        return after(x, *self.last)

    def wait(self, *values):
        self.last += values


def norm_kernel(x_ref, seg_ref, gain_ref, shift_ref, out_ref):
    size, width = x_ref.shape
    hat, _ = standardized(x_ref[...].astype(F32))
    out_ref[:size] = (hat * gain_ref[...] + shift_ref[...]).astype(BF)
    ids = jnp.broadcast_to(seg_ref[...].astype(F32), (16, size)).astype(BF)
    out_ref[size:, :size] = ids
    out_ref[size:, size:] = jnp.zeros((16, width - size), BF)


def masks_kernel(cot_ref, seg_ref, out_ref):
    out_ref[...] = jnp.where(seg_ref[...] != 0, cot_ref[...], jnp.zeros((), BF))


def qkv_kernel(r0, heads, t_ref, n0, n1, w_ref, *refs):
    size = n0.shape[0] - 16
    t = t_ref[0]
    q_ref, k_ref, v_ref = refs[-3:]
    base_row = 0
    if len(refs) > 3:
        mine = pl.ds(pl.multiple_of((t >> 1) * (2 * size), size), 2 * size)
        for given, out_ref in zip(refs[:3], refs[3:]):
            out_ref[:, mine, :] = given[...]
        base_row = ((t >> 1) ^ 1) * (2 * size)
    lane = lax.broadcasted_iota(jnp.int32, (size, HD), 1)
    row = lax.broadcasted_iota(jnp.int32, (size, HD), 0)
    article = (lane >= 3) & (lane < 7)
    v_more = jnp.where(lane < 3, 1.0, 0.0).astype(BF)
    for r, n_ref in ((r0, n0), (r0 + 1, n1)):
        n = n_ref[:size]
        place = ((t ^ r) * size + row).astype(F32)
        ids = jnp.broadcast_to(n_ref[size:, :size].astype(F32)[:1], (HD, size)).T
        hot = ids == (lane - 3).astype(F32)
        q_more = jnp.where((lane < 3) | (article & hot), 1.0, 0.0).astype(BF)
        base = jnp.where(article, jnp.where(hot, 0.0, NEG), jnp.where((lane >= 7) & (lane < 10), 1.0, 0.0))
        q = (dot(n, w_ref[0]) * (HD**-0.5 * LOG2E)).astype(BF)
        k = dot(n, w_ref[1]).astype(BF)
        v = dot(n, w_ref[2]).astype(BF)
        at = pl.ds(pl.multiple_of(base_row + ((t ^ r) & 1) * size, size), size)
        for h in range(heads):
            power = jnp.full((size, HD), (t * heads + h + 1).astype(F32) * (-8.0 / H), F32)
            hi, mid, lo = split3(jnp.exp2(power) * LOG2E * place)
            more = jnp.where(lane == 0, hi, jnp.where(lane == 1, mid, jnp.where(lane == 2, lo, base.astype(BF))))
            sl = slice(h * HD, (h + 1) * HD)
            q_ref[h, at, :HD] = q[:, sl]
            q_ref[h, at, HD:] = q_more
            k_ref[h, at, :HD] = k[:, sl]
            k_ref[h, at, HD:] = more
            v_ref[h, at, :HD] = v[:, sl]
            v_ref[h, at, HD:] = v_more


def attn_fwd_kernel(t_ref, q_ref, k_ref, v_ref, m0, m1, m2, m3, xa_ref, xb_ref, kept):
    heads, length, _ = q_ref.shape
    half = length // 8
    t = t_ref[0]
    row = lax.broadcasted_iota(jnp.int32, (half, half), 0)
    col = lax.broadcasted_iota(jnp.int32, (half, half), 1)
    keep = col <= row
    lane = lax.broadcasted_iota(jnp.int32, (half, HD), 1)
    for block in range(8):
        p, u = block // 2, block % 2
        start = block * half
        end = start + half
        for h in range(heads):
            q = q_ref[h, start:end, :]
            near = jnp.where(keep, dot(q, k_ref[h, start:end, :], NT), NEG)
            top = jnp.max(near, -1, keepdims=True)
            if start:
                far = dot(q, k_ref[h, :start, :], NT)
                top = jnp.maximum(top, jnp.max(far, -1, keepdims=True))
            out = dot(jnp.exp2(near - top).astype(BF), v_ref[h, start:end, :])
            if start:
                out = out + dot(jnp.exp2(far - top).astype(BF), v_ref[h, :start, :])
            total = out[:, HD : HD + 1]
            kept[p ^ t, u * half : (u + 1) * half, h * HD : (h + 1) * HD] = (out[:, :HD] / total).astype(BF)
            hi, mid, lo = split3(-(top + jnp.log2(total)))
            more = jnp.where(lane == 7, hi, jnp.where(lane == 8, mid, jnp.where(lane == 9, lo, q[:, HD:])))
            (xa_ref, xb_ref)[u][h, p] = more
    for r, out_ref in enumerate((m0, m1, m2, m3)):
        out_ref[...] = kept[r]


def attn_fwd(order, t, q, k, v):
    heads, length, _ = q.shape
    size = length // 4
    outs = [arr((size, heads * HD))] * 4 + [arr((heads, 4, size // 2, HD))] * 2
    scratch = [pltpu.VMEM((4, size, heads * HD), BF)]
    return order("attn_fwd", attn_fwd_kernel, outs, (t, q, k, v), limit=10, scratch=scratch, scalars=1)


def attn_bwd_kernel(u, t_ref, q_ref, k_ref, v_ref, x_ref, *rest):
    do_refs, o_refs, rest = rest[:4], rest[4:8], rest[8:]
    heads, length, _ = q_ref.shape
    half = length // 8
    pick = lambda ref, sl: ref[u * half : (u + 1) * half, sl]
    size = 2 * half
    width = heads * HD
    if u == 0:
        dq_ref, dk_ref, dv_ref, qs, ds, dqt = rest
    else:
        dq_first, dk_first, dv_first, g_ref, qs, ds, dqt = rest
    t = t_ref[0]
    lane = lax.broadcasted_iota(jnp.int32, (half, HD), 1)
    for h in range(heads):
        sl = slice(h * HD, (h + 1) * HD)
        for p in range(4):
            qs[h, p, :, :HD] = q_ref[h, (2 * p + u) * half : (2 * p + u + 1) * half, :HD]
            qs[h, p, :, HD:] = x_ref[h, p]
        for r in range(4):
            do = pick(do_refs[r], sl) if r == 1 else do_refs[r][:half, sl]
            delta = jnp.sum(do.astype(F32) * pick(o_refs[r], sl).astype(F32), -1, keepdims=True)
            hi, mid, lo = split3(-delta)
            ds[h, r ^ t, :, :HD] = do
            ds[h, r ^ t, :, HD:] = jnp.where(
                lane == 0, hi, jnp.where(lane == 1, mid, jnp.where(lane == 2, lo, jnp.zeros_like(hi)))
            )
    near_rows = half * (1 + u)
    row = lax.broadcasted_iota(jnp.int32, (near_rows, half), 0)
    col = lax.broadcasted_iota(jnp.int32, (near_rows, half), 1)
    keep = row <= col + u * half
    for p in range(4):
        for h in range(heads):

            def part(rows, first, last, masked):
                at = slice(p * size, p * size + rows)
                n = (last - first) * half
                q = qs[h, first:last].reshape(n, 2 * HD)
                do = ds[h, first:last].reshape(n, 2 * HD)
                s = dot(k_ref[h, at, :], q, NT)
                if masked:
                    s = jnp.where(keep, s, NEG)
                e = jnp.exp2(s)
                de = (e * dot(v_ref[h, at, :], do, NT)).astype(BF)
                dv = dot(e.astype(BF), do[:, :HD])
                dk = dot(de, q[:, :HD])
                dq = dot(k_ref[h, at, :HD], de, TN)
                cols = slice(first * half, last * half)
                if p:
                    dqt[h, :, cols] += dq
                else:
                    dqt[h, :, cols] = dq
                return dk, dv

            dk, dv = part(near_rows, p, p + 1, True)
            if p < 3:
                dk_far, dv_far = part(size, p + 1, 4, False)
                if near_rows < size:
                    pad = jnp.zeros((size - near_rows, HD), F32)
                    dk, dv = jnp.concatenate([dk, pad]), jnp.concatenate([dv, pad])
                dk, dv = dk + dk_far, dv + dv_far
            elif near_rows < size:
                pad = jnp.zeros((size - near_rows, HD), F32)
                dk, dv = jnp.concatenate([dk, pad]), jnp.concatenate([dv, pad])
            dq = (dqt[h, :, p * half : (p + 1) * half].T * HD**-0.5).astype(BF)
            sl = slice(h * HD, (h + 1) * HD)
            if u == 0:
                dk_ref[h, p * size : (p + 1) * size] = dk
                dv_ref[h, p * size : (p + 1) * size] = dv
                dq_ref[p ^ t, :, sl] = dq
            else:
                at = slice(p * size, (p + 1) * size)
                g_ref[p ^ t, half:, sl] = dq
                g_ref[p ^ t, :, width + h * HD : width + (h + 1) * HD] = (
                    (dk + dk_first[h, at]) * (1.0 / LOG2E)
                ).astype(BF)
                g_ref[p ^ t, :, 2 * width + h * HD : 2 * width + (h + 1) * HD] = (dv + dv_first[h, at]).astype(BF)
    if u == 1:
        for r in range(4):
            g_ref[r, :half, :width] = dq_first[r]


def attn_bwd(order, u, t, q, k, v, x, do, o, first=()):
    heads, length, _ = q.shape
    half = length // 8
    width = heads * HD
    if u == 0:
        outs = [arr((4, half, width)), arr((heads, length, HD), F32), arr((heads, length, HD), F32)]
    else:
        outs = [arr((4, 2 * half, 3 * width))]
    return order(
        "attn_bwd",
        functools.partial(attn_bwd_kernel, u),
        outs,
        (t, q, k, v, x, *do, *o, *first),
        limit=16,
        scratch=[pltpu.VMEM((heads, 4, half, 2 * HD), BF)] * 2 + [pltpu.VMEM((heads, HD, 4 * half), F32)],
        scalars=1,
    )


def out_kernel(m0, m1, m2, m3, w0, w1, w2, w3, x_ref, bias_ref, gain_ref, shift_ref, resid_ref, n_ref, na_ref, nb_ref):
    half = na_ref.shape[0]
    for u, half_ref in enumerate((na_ref, nb_ref)):
        at = slice(u * half, (u + 1) * half)
        total = sum(dot(m[at], w[...]) for m, w in ((m0, w0), (m1, w1), (m2, w2), (m3, w3)))
        resid = x_ref[at, :].astype(F32) + (total + bias_ref[...])
        resid_ref[at] = resid
        hat, _ = standardized(resid)
        n = (hat * gain_ref[...] + shift_ref[...]).astype(BF)
        n_ref[at] = n
        half_ref[...] = n


def up_kernel(n0, n1, up_ref, act_ref, slope_ref):
    c = 0.7978845608028654
    rows = n0.shape[0]
    step = min(rows, 256)
    for i, n_ref in enumerate((n0, n1)):
        for first in range(0, rows, step):
            at = slice(i * rows + first, i * rows + first + step)
            v = dot(n_ref[first : first + step], up_ref[...])
            square = v * v
            th = jnp.tanh(v * (c + (c * 0.044715) * square))
            half_v = 0.5 * v
            act_ref[at] = (half_v + half_v * th).astype(BF)
            slope_ref[at] = (0.5 + 0.5 * th + half_v * (1.0 - th * th) * (c + (3 * c * 0.044715) * square)).astype(BF)


def back_kernel(u, g0, g1, slope_ref, up_ref, down_ref, dpre_ref, p0, p1):
    rows = p0.shape[0]
    step = min(rows, 256)
    for i, (g_ref, out_ref) in enumerate(((g0, p0), (g1, p1))):
        for first in range(0, rows, step):
            at = slice(i * rows + first, i * rows + first + step)
            g = g_ref[u * rows + first : u * rows + first + step]
            dpre = (dot(g, down_ref[...], NT) * slope_ref[at].astype(F32)).astype(BF)
            dpre_ref[at] = dpre
            out_ref[first : first + step] = dot(dpre, up_ref[...], NT).astype(BF)


def down_kernel(sources, *refs):
    count = max(i for i, _ in sources) + 1
    acts, w_ref, outs = refs[:count], refs[count], refs[count + 1 :]
    half = outs[0].shape[0] // 2
    for n, (i, first) in enumerate(sources):
        out = dot(acts[i][first : first + half], w_ref[...]).astype(BF)
        outs[n // 2][n % 2 * half : (n % 2 + 1) * half] = out


def mid_kernel(u, *refs):
    if u:
        before, refs = refs[0], refs[1:]
    p0, c1, y2, resid_ref, cot_ref, seg_ref, gain_ref, w0, w1, w2, w3, dresid_ref, dattn_ref, m0, m1, m23, sums_ref = refs
    half = y2.shape[0]
    sl = slice(u * half, (u + 1) * half)
    grad = p0[sl].astype(F32) + c1[sl].astype(F32) + y2[...].astype(F32)
    hat, inverse = standardized(resid_ref[sl])
    g = jnp.where(seg_ref[sl] != 0, cot_ref[sl].astype(F32), 0.0)
    dresid = g + norm_back(grad, gain_ref[...], hat, inverse)
    dresid_ref[...] = dresid
    dattn = dresid.astype(BF)
    dattn_ref[...] = dattn
    m0[...] = dot(dattn, w0[...], NT).astype(BF)
    if u:
        m1[:half] = before[...]
    m1[u * half :] = dot(dattn, w1[...], NT).astype(BF)
    m23[:half] = dot(dattn, w2[...], NT).astype(BF)
    m23[half:] = dot(dattn, w3[...], NT).astype(BF)
    rows = [grad * hat, grad, dresid, g]
    sums_ref[...] = jnp.concatenate([jnp.sum(v, 0, keepdims=True) for v in rows] + [jnp.zeros((4, hat.shape[1]), F32)])


def dn1_kernel(pair, g_ref, w_ref, a_ref, b_ref):
    width = w_ref.shape[2]
    for r, out_ref in ((2 * pair, a_ref), (2 * pair + 1, b_ref)):
        out_ref[...] = sum(dot(g_ref[r, :, c * width : (c + 1) * width], w_ref[c], NT) for c in range(3)).astype(BF)


def last_kernel(p0, c1, y2, x_ref, da, db, gain_ref, out_ref):
    grad = p0[...].astype(F32) + c1[...].astype(F32) + y2[...].astype(F32)
    hat, inverse = standardized(x_ref[...].astype(F32))
    dresid = jnp.where(pl.program_id(0) < 2, da[...], db[...])
    out_ref[...] = dresid + norm_back(grad, gain_ref[...], hat, inverse)


def result_kernel(resid_ref, p0, c1, y2, seg_ref, bias_ref, out_ref):
    total = p0[...].astype(F32) + c1[...].astype(F32) + y2[...].astype(F32)
    out_ref[...] = jnp.where(seg_ref[...] != 0, resid_ref[...] + total + bias_ref[...], 0.0).astype(BF)


def quarters(kinds, size, width):
    rows = size // 4
    maps = {
        "w": lambda i: (i, 0),
        "a": lambda i: (jnp.minimum(i, 1), 0),
        "b": lambda i: (jnp.maximum(i - 2, 0), 0),
        "r": lambda i: (0, 0),
        "s": lambda i: (i, 0),
    }
    specs = [pl.BlockSpec((1 if k == "r" else rows, 1 if k == "s" else width), maps[k]) for k in kinds]
    return specs[:-1], (specs[-1],), (4,)


def order_of(bits):
    rest = [0]
    for bit in reversed(bits[1:]):
        rest = [e | (1 << bit) for e in rest] + rest
    return [e | (1 << bits[0]) for e in rest], rest


def ffn_grad_kernel(bits, tile, count, pairs, d_ref, *refs):
    lefts, rights, outs = refs[:count], refs[count:-2], refs[-2:]
    for out_ref, blocks in zip(outs, order_of(bits)):
        for i, e in enumerate(blocks):
            cols = pl.ds(bits_of(d_ref[0], e, tile), tile)
            total = 0.0
            for left, first, rows, right, at in pairs:
                total += dot(lefts[left][first : first + rows, cols], rights[right][at : at + rows], TN)
            out_ref[i] = total.astype(BF)


def ffn_grad(order, name, bits, d, lefts, rights, pairs):
    tile = lefts[0].shape[1] // 8
    body = functools.partial(ffn_grad_kernel, bits, tile, len(lefts), pairs)
    return order(name, body, [arr((4, tile, rights[0].shape[1]))] * 2, (d, *lefts, *rights), scalars=1)


def out_grad_kernel(tile, d_ref, la, lb, m0, m1, m2, m3, send_ref, keep_ref):
    half, width = la.shape[0], m0.shape[1]
    for e in range(8):
        cols = pl.ds(bits_of(d_ref[0], e, tile), tile)
        for r, m in enumerate((m0, m1, m2, m3)):
            total = (dot(la[:, cols], m[:half], TN) + dot(lb[:, cols], m[half:], TN)).astype(BF)
            out_ref = send_ref if r % 2 else keep_ref
            out_ref[e, :, (r // 2) * width : (r // 2 + 1) * width] = total


def split_add_kernel(bits, a_ref, b_ref, *outs):
    for out_ref, blocks in zip(outs, order_of(bits)):
        for i, e in enumerate(blocks):
            out_ref[i] = (a_ref[e].astype(F32) + b_ref[e].astype(F32)).astype(BF)


def qkv_grad_kernel(orders, tile, d_ref, n0, n1, n2, n3, g_ref, w_ref, sums_a, sums_b, gain_ref, shift_ref, *refs):
    outs, kept, lines = refs[:4], refs[4], refs[5]
    width = w_ref.shape[2]
    size = g_ref.shape[1]
    count = jnp.ones((8, size), BF)
    weighted, shifted = 0.0, 0.0
    for c in range(3):
        sl = slice(c * width, (c + 1) * width)
        total = sum(dot(n[:size, :], g_ref[r, :, sl], TN) for r, n in enumerate((n0, n1, n2, n3)))
        for s in range(8):
            kept[s ^ d_ref[0], :, sl] = total[s * tile : (s + 1) * tile].astype(BF)
        w = w_ref[c].astype(F32)
        weighted += total * w
        shifted += sum(dot(count, g_ref[r, :, sl]) for r in range(4))[:1] * w
    ones = jnp.ones((8, width), F32)
    high = lambda v: lax.dot_general(ones, v, NT, precision=lax.Precision.HIGHEST, preferred_element_type=F32)
    shift_sum = high(shifted)[:1]
    gain_sum = (high(weighted)[:1] - shift_ref[...] * shift_sum) / gain_ref[...]
    both = sums_a[...] + sums_b[...]
    rows = jnp.concatenate([gain_sum, shift_sum, both[:4], jnp.zeros((10, both.shape[1]), F32)]).astype(BF)
    for s in range(8):
        lines[s ^ d_ref[0]] = rows[:, s * tile : (s + 1) * tile]
    part = outs[0].shape[2]
    for m, bits in enumerate(orders):
        for k, blocks in enumerate(order_of(bits)):
            for i, e in enumerate(blocks):
                outs[2 * m + k][i, :tile] = kept[e, :, m * part : (m + 1) * part]
                outs[2 * m + k][i, tile:] = jnp.zeros((16, part), BF)
                if m == 0:
                    outs[k][i, tile:, :tile] = lines[e]


def add_kernel(a_ref, b_ref, out_ref):
    rows = out_ref.shape[0]
    out_ref[...] = (a_ref[...].astype(F32) + b_ref[b_ref.shape[0] - rows :].astype(F32)).astype(BF)


def stage_kernel(turned, groups, later, *refs):
    count = len(turned)
    own, got, outs = refs[:count], refs[count : count + len(groups)], refs[count + len(groups) :]
    total = [None] * count
    for ref, group in zip(got, groups):
        at = 0
        for m in group:
            width = own[m].shape[2]
            total[m] = own[m][...].astype(F32) + ref[:, :, at : at + width].astype(F32)
            at += width
    if not later:
        for m in range(count):
            outs[m][...] = total[m][0].T if turned[m] else total[m][0]
        return
    for ref, group in zip(outs[count:], later):
        at = 0
        for m in group:
            blocks, _, width = total[m].shape
            outs[m][...] = total[m][blocks // 2 :].astype(BF)
            ref[:, :, at : at + width] = total[m][: blocks // 2].astype(BF)
            at += width


def after(x, *others):
    return lax.optimization_barrier((x, *others))[0]


def to_core(x):
    return lax.ppermute(x, "tensor", [(i, i ^ 1) for i in range(4)])


def to_chip(x):
    return lax.ppermute(x, "tensor", [(i, i ^ 2) for i in range(4)])


def to_diag(x):
    return lax.ppermute(x, "tensor", [(i, i ^ 3) for i in range(4)])


def gather(x):
    far = to_chip(x)
    return [x, to_core(x), far, to_core(far)]


class Reduce:
    def __init__(self, order, dp, d, *matrices):
        self.order, self.dp, self.d = order, dp, d
        self.low = dp.bit_length() - 4
        self.own = [parts[1] for parts, _, _ in matrices]
        self.bits = [list(bits[1:]) for _, bits, _ in matrices]
        self.turned = [turned for _, _, turned in matrices]
        self.groups = [[m] for m in range(len(matrices))]
        self.got = [self.swap(parts[0], bits[0]) for parts, bits, _ in matrices]

    def merge(self, other):
        count = len(self.own)
        self.own, self.bits, self.turned = self.own + other.own, self.bits + other.bits, self.turned + other.turned
        self.groups, self.got = self.groups + [[m + count for m in g] for g in other.groups], self.got + other.got

    def swap(self, x, bit):
        return lax.ppermute(x, "dp", [(i, i ^ (1 << (bit + self.low))) for i in range(self.dp)])

    def stage(self):
        count = len(self.own)
        turned = [bool(f) and not self.low for f in self.turned]
        later = []
        if self.bits[0]:
            for bit in range(3):
                group = [m for m in range(count) if self.bits[m][0] == bit]
                later += [group] if group else []
            outs = [arr((own.shape[0] // 2, *own.shape[1:])) for own in self.own]
            for group in later:
                blocks, rows, _ = outs[group[0]].shape
                outs.append(arr((blocks, rows, sum(self.own[m].shape[2] for m in group))))
        else:
            shapes = [own.shape for own in self.own]
            outs = [arr((s[2], s[1]) if f else s[1:], F32) for s, f in zip(shapes, turned)]
        body = functools.partial(stage_kernel, turned, self.groups, later)
        sums = self.order("stage", body, outs, (*self.own, *self.got))
        if not later:
            return [s if f is None else self.rest(s, f) for s, f in zip(sums, self.turned)]
        self.own = list(sums[:count])
        self.got = [self.swap(x, self.bits[group[0]][0]) for x, group in zip(sums[count:], later)]
        self.groups, self.bits = later, [bits[1:] for bits in self.bits]
        return None

    def rest(self, total, turned):
        for bit in range(self.low - 1, -1, -1):
            mine = (self.d >> bit) & 1
            view = total.reshape(2, total.shape[0] // 2, total.shape[1])
            send = lax.dynamic_index_in_dim(view, 1 - mine, 0, keepdims=False)
            keep = lax.dynamic_index_in_dim(view, mine, 0, keepdims=False)
            total = keep + lax.ppermute(send, "dp", [(i, i ^ (1 << bit)) for i in range(self.dp)])
        return total.T if turned and self.low else total


def place_kernel(rows, d_ref, in_ref, out_ref):
    for i in range(8):
        e = (i & 1) << 2 | (i & 2) | i >> 2
        out_ref[pl.ds(bits_of(d_ref[0], e, rows), rows)] = in_ref[i * rows : (i + 1) * rows]


def local(dp, block_input, segment_ids, w_qkv, w_out, w_up, w_down, ln1_gain, ln1_bias, ln2_gain, ln2_bias, out_bias, down_bias, cotangent):
    size, width = block_input.shape[1:]
    half = size // 2
    hidden = w_up.shape[1]
    local_width = w_qkv.shape[2]
    heads = local_width // HD
    t = lax.axis_index("tensor")
    d = lax.axis_index("dp")
    low = dp.bit_length() - 4
    t_arg = t[None].astype(jnp.int32)
    block_arg = (d >> low)[None].astype(jnp.int32)
    x = block_input[0]
    cot = cotangent[0]
    seg = segment_ids[0][:, None]
    gain1, shift1, gain2, shift2 = ln1_gain[None], ln1_bias[None], ln2_gain[None], ln2_bias[None]
    token = (size, width)
    chunk = (half, width)
    order = Order()

    part = local_width // 8
    wo_part = to_chip(lax.dynamic_slice_in_dim(w_out, (d >> low) * part, part, 0))
    order.wait(wo_part)
    (n1_own,) = order("norm", norm_kernel, [arr((size + 16, width))], (x, segment_ids, gain1, shift1))
    n1_far, n1_core = to_chip(n1_own), to_core(n1_own)

    def spread(x, bit):
        sent = lax.ppermute(x, "dp", [(i, i ^ (1 << (bit + low))) for i in range(dp)])
        return jnp.concatenate([x, sent])

    wo_part = spread(order.then(wo_part), 2)
    (dffn_own,) = order("masks", masks_kernel, [arr(token)], (cot, seg))
    dffn_core = to_core(dffn_own)
    half_row = [arr((heads, 2 * size, 2 * HD))] * 3
    near = order("qkv", functools.partial(qkv_kernel, 0, heads), half_row, (t_arg, n1_own, n1_core, w_qkv), scalars=1)
    order.wait(dffn_core)
    wo_part = spread(spread(order.then(wo_part), 1), 0)
    body = functools.partial(place_kernel, part)
    (wo_far,) = order("place", body, [arr(w_out.shape)], (block_arg, wo_part), scalars=1)
    wo = [w_out, to_core(order.then(w_out)), wo_far, to_core(wo_far)]
    n1 = [n1_own, n1_core, n1_far, to_core(order.then(n1_far))]
    dffn_far = to_chip(after(dffn_own, n1_far))
    order.wait(wo[1], wo[3])
    args = (t_arg, n1[2], n1[3], w_qkv, *near)
    row = [arr((heads, 4 * size, 2 * HD))] * 3
    q, k, v = order("qkv", functools.partial(qkv_kernel, 2, heads), row, args, scalars=1)

    *o, x_a, x_b = attn_fwd(order, t_arg, q, k, v)
    mixed = [o[0], to_core(o[1]), to_chip(o[2]), to_diag(o[3])]
    args = (*mixed, *wo, x, out_bias[None], gain2, shift2)
    resid, n2_own, n2_a, n2_b = order("out_proj", out_kernel, [arr(token, F32), arr(token)] + [arr(chunk)] * 2, args)
    n2_a = to_chip(n2_a)
    n2_core = to_core(n2_own)
    n2_b = to_chip(n2_b)
    dffn = [dffn_own, dffn_core, dffn_far, to_core(order.then(dffn_far))]
    order.wait(dffn[3])

    def up(first, second):
        outs = [arr((2 * first.shape[0], hidden))] * 2
        return order("up", up_kernel, outs, (first, second, w_up))

    def back(u, grads, slope):
        rows = slope.shape[0] // 2
        outs = [arr(slope.shape)] + [arr((rows, width))] * 2
        return order("back", functools.partial(back_kernel, u), outs, (*grads, slope, w_up, w_down))

    act_near, slope = up(n2_own, n2_core)
    dpre_near, p0, p1 = back(0, dffn[:2], slope)
    p1 = to_core(p1)
    n2_a = [n2_a, to_core(order.then(n2_a))]
    order.wait(p1)
    act_a, slope = up(*n2_a)
    dpre_a, p2, send_a = back(0, dffn[2:], slope)
    send_a = to_core(send_a)
    n2_b = [n2_b, to_core(order.then(n2_b))]
    act_b, slope = up(*n2_b)
    (chip,) = order("add", add_kernel, [arr(chunk)], (p2, send_a))
    chip_a = to_chip(chip)
    dpre_b, p2, send_b = back(1, dffn[2:], slope)
    send_b = to_core(send_b)
    body = functools.partial(down_kernel, [(0, i * half) for i in range(4)])
    ffn0, ffn1 = order("down", body, [arr(token)] * 2, (act_near, w_down))
    (chip,) = order("add", add_kernel, [arr(chunk)], (p2, send_b))
    chip_b = to_chip(chip)
    ffn1 = to_core(order.then(ffn1))
    body = functools.partial(down_kernel, [(0, 0), (1, 0), (0, half), (1, half)])
    ffn2, ffn3 = order("down", body, [arr(token)] * 2, (act_a, act_b, w_down))
    ffn3 = to_core(ffn3)
    order.wait(ffn1)

    def middle(u, y2, before=()):
        piece = (half, local_width)
        both = (2 * half, local_width)
        outs = [arr(chunk, F32), arr(chunk), arr(piece), arr(both if u else piece), arr(both), arr((8, width), F32)]
        args = (*before, p0, p1, y2, resid, cot, seg, gain2, *wo)
        return order("mid", functools.partial(mid_kernel, u), outs, args)

    bits = ((0, 1, 2), (1, 0, 2))
    pairs = [(0, 0, size, 0, 0), (1, 0, size, 0, size)]
    pairs += [(2 + 2 * u + i, 0, half, 1 + u, i * half) for u in range(2) for i in range(2)]
    rights = [dpre_near, dpre_a, dpre_b]
    parts = ffn_grad(order, "up_grad", bits[0], block_arg, [n2_own, n2_core, *n2_a, *n2_b], rights, pairs)
    up_reduce = Reduce(order, dp, d, (parts, bits[0], False))
    (ffn_chip,) = order("add", add_kernel, [arr(token)], (ffn2, ffn3))
    dresid_a, dattn_a, m0a, m1a, send_a, sums_a = middle(0, chip_a)
    far_a = to_chip(send_a)
    pairs = [(0, 0, size, 0, 0), (1, 0, size, 0, size)]
    pairs += [(2 + i, u * half, half, 1 + u, i * half) for u in range(2) for i in range(2)]
    parts = ffn_grad(order, "down_grad", bits[1], block_arg, dffn, [act_near, act_a, act_b], pairs)
    down_reduce = Reduce(order, dp, d, (parts, bits[1], True))
    dresid_b, dattn_b, m0b, m1b, send_b, sums_b = middle(1, chip_b, (m1a,))
    core_ab = to_core(m1b)
    far_b = to_chip(send_b)
    tile = width // 8
    outs = [arr((8, tile, 2 * local_width))] * 2
    args = (block_arg, dattn_a, dattn_b, *mixed)
    out_send, out_keep = order("out_grad", functools.partial(out_grad_kernel, tile), outs, args, scalars=1)

    diag_a = to_core(after(order.then(far_a[half:]), core_ab))
    do = (m0a, core_ab, far_a, diag_a)
    first = attn_bwd(order, 0, t_arg, q, k, v, x_a, do, o)
    ffn_chip = to_chip(order.then(ffn_chip))
    out_send = to_core(order.then(out_send))
    diag_b = to_core(order.then(far_b[half:]))
    up_reduce.stage()
    do = (m0b, core_ab, far_b, diag_b)
    (dqkv,) = attn_bwd(order, 1, t_arg, q, k, v, x_b, do, o, first)
    down_reduce.stage()
    own, send = order("dn1", functools.partial(dn1_kernel, 1), [arr(token)] * 2, (dqkv, w_qkv))
    send = to_core(send)
    dn1_own, dn1_send = order("dn1", functools.partial(dn1_kernel, 0), [arr(token)] * 2, (dqkv, w_qkv))
    (chip,) = order("add", add_kernel, [arr(token)], (own, send))
    dn1_chip = to_chip(chip)
    outs = [arr((4, tile, 2 * local_width))] * 2
    parts = order("split", functools.partial(split_add_kernel, bits[0]), outs, (out_keep, out_send))
    out_reduce = Reduce(order, dp, d, (parts, bits[0], False))
    cols = 3 * local_width // 2
    outs = [arr((4, tile + 16, cols))] * 4
    args = (block_arg, *n1, dqkv, w_qkv, sums_a, sums_b, gain1, shift1)
    scratch = [pltpu.VMEM((8, tile, 2 * cols), BF), pltpu.VMEM((8, 16, tile), BF)]
    body = functools.partial(qkv_grad_kernel, bits, tile)
    parts = order("qkv_grad", body, outs, args, scratch=scratch, scalars=1)
    up_reduce.merge(down_reduce)
    up_reduce.stage()
    args = (resid, ffn0, ffn1, ffn_chip, seg, down_bias[None])
    (output,) = order("result", result_kernel, [arr(token)], args, blocks=quarters("wwwwsrw", *token))
    parts = [order.then(parts[0]), parts[1], order.then(parts[2]), parts[3]]
    qkv_reduce = Reduce(order, dp, d, (parts[:2], bits[0], None), (parts[2:], bits[1], None))
    out_reduce.stage()
    qkv_reduce.stage()
    up_sum, down_sum = up_reduce.stage()
    out_reduce.stage()
    dn1_core = to_core(order.then(dn1_send))
    qkv_reduce.stage()
    blocks = quarters("wwwwabrw", *token)
    args = (dn1_own, dn1_core, dn1_chip, x, dresid_a, dresid_b, gain1)
    (x_grad,) = order("last", last_kernel, [arr(token, F32)], args, blocks=blocks)
    (out_sum,) = out_reduce.stage()
    out_sum = out_sum[:, :local_width] + to_chip(order.then(out_sum[:, local_width:]))
    first, second = qkv_reduce.stage()
    lines = qkv_reduce.rest(first[tile : tile + 6, :tile].T, False)
    lines = lines + to_core(lines)
    lines = lines + to_chip(lines)
    chunk = width // dp // 4
    vectors = lax.dynamic_slice_in_dim(lines, t * chunk, chunk, 0)
    qkv_sum = jnp.concatenate([qkv_reduce.rest(p[:tile], False) for p in (first, second)], 1)
    qkv_sum = qkv_sum.reshape(width // dp, 3, local_width).transpose(1, 0, 2)
    return (output[None], x_grad[None], qkv_sum, out_sum.T, up_sum, down_sum, *(vectors[:, i] for i in range(6)))


def solution(mesh):
    row = P("dp", "tensor", None)
    matrix = (P(None, None, "tensor"), P("tensor", None), P(None, "tensor"), P("tensor", None))
    in_specs = (row, P("dp", "tensor"), *matrix) + (P(),) * 6 + (row,)
    vector = P(("dp", "tensor"))
    out_specs = (row, row, P(None, "dp", "tensor"), P("tensor", "dp"), P("dp", "tensor"), P("tensor", "dp")) + (vector,) * 6
    run = functools.partial(local, mesh.shape["dp"])
    return jax.shard_map(run, mesh=mesh, in_specs=in_specs, out_specs=out_specs, check_vma=False)
```

```python
import functools

import jax
import jax.numpy as jnp
from jax import lax
from jax.experimental import pallas as pl
from jax.experimental.pallas import tpu as pltpu
from jax.sharding import PartitionSpec as P

H = 8
HD = 128
EPS = 1e-05
NEG = -1e30
LOG2E = 1.4426950408889634
BF = jnp.bfloat16
F32 = jnp.float32
NN = (((1,), (0,)), ((), ()))
NT = (((1,), (1,)), ((), ()))
TN = (((0,), (0,)), ((), ()))
VMEM = pl.BlockSpec(memory_space=pltpu.VMEM)
SMEM = pl.BlockSpec(memory_space=pltpu.SMEM)


def dot(a, b, dims=NN):
    return lax.dot_general(a, b, dims, preferred_element_type=F32)


def call(name, body, outs, args, limit=12, scratch=(), scalars=0, blocks=None):
    in_specs, out_specs, grid = blocks or ([SMEM] * scalars + [VMEM] * (len(args) - scalars), (VMEM,) * len(outs), ())
    return pl.pallas_call(
        body,
        out_shape=tuple(outs),
        grid=grid,
        in_specs=in_specs,
        out_specs=out_specs,
        scratch_shapes=list(scratch),
        name=name,
        cost_estimate=pl.CostEstimate(flops=1, bytes_accessed=1, transcendentals=0),
        compiler_params=pltpu.CompilerParams(vmem_limit_bytes=limit * 2**20),
    )(*args)


def arr(shape, dtype=BF):
    return jax.ShapeDtypeStruct(shape, dtype)


def split3(v):
    hi = v.astype(BF)
    rest = v - hi.astype(F32)
    mid = rest.astype(BF)
    return hi, mid, (rest - mid.astype(F32)).astype(BF)


def standardized(values):
    center = values - jnp.mean(values, -1, keepdims=True)
    inverse = lax.rsqrt(jnp.mean(center * center, -1, keepdims=True) + EPS)
    return center * inverse, inverse


def norm_back(grad, gain, hat, inverse):
    e = grad * gain
    return (e - jnp.mean(e, -1, keepdims=True) - hat * jnp.mean(e * hat, -1, keepdims=True)) * inverse


def bits_of(index, place, value):
    return pl.multiple_of((index ^ place) * value, value)


class Order:
    def __init__(self):
        self.last = ()

    def __call__(self, name, body, outs, args, limit=12, scratch=(), scalars=0, blocks=None):
        args = list(args)
        if self.last:
            args[scalars] = after(args[scalars], *self.last)
        got = call(name, body, outs, args, limit, scratch, scalars, blocks)
        self.last = (got[-1],)
        return got

    def then(self, x):
        return after(x, *self.last)

    def wait(self, *values):
        self.last += values


def norm_kernel(x_ref, seg_ref, gain_ref, shift_ref, out_ref):
    size, width = x_ref.shape
    hat, _ = standardized(x_ref[...].astype(F32))
    out_ref[:size] = (hat * gain_ref[...] + shift_ref[...]).astype(BF)
    ids = jnp.broadcast_to(seg_ref[...].astype(F32), (16, size)).astype(BF)
    out_ref[size:, :size] = ids
    out_ref[size:, size:] = jnp.zeros((16, width - size), BF)


def masks_kernel(cot_ref, seg_ref, out_ref):
    out_ref[...] = jnp.where(seg_ref[...] != 0, cot_ref[...], jnp.zeros((), BF))


def qkv_kernel(r0, heads, t_ref, n0, n1, w_ref, *refs):
    size = n0.shape[0] - 16
    t = t_ref[0]
    q_ref, k_ref, v_ref = refs[-3:]
    base_row = 0
    if len(refs) > 3:
        mine = pl.ds(pl.multiple_of((t >> 1) * (2 * size), size), 2 * size)
        for given, out_ref in zip(refs[:3], refs[3:]):
            out_ref[:, mine, :] = given[...]
        base_row = ((t >> 1) ^ 1) * (2 * size)
    lane = lax.broadcasted_iota(jnp.int32, (size, HD), 1)
    row = lax.broadcasted_iota(jnp.int32, (size, HD), 0)
    article = (lane >= 3) & (lane < 7)
    v_more = jnp.where(lane < 3, 1.0, 0.0).astype(BF)
    for r, n_ref in ((r0, n0), (r0 + 1, n1)):
        n = n_ref[:size]
        place = ((t ^ r) * size + row).astype(F32)
        ids = jnp.broadcast_to(n_ref[size:, :size].astype(F32)[:1], (HD, size)).T
        hot = ids == (lane - 3).astype(F32)
        q_more = jnp.where((lane < 3) | (article & hot), 1.0, 0.0).astype(BF)
        base = jnp.where(article, jnp.where(hot, 0.0, NEG), jnp.where((lane >= 7) & (lane < 10), 1.0, 0.0))
        q = (dot(n, w_ref[0]) * (HD**-0.5 * LOG2E)).astype(BF)
        k = dot(n, w_ref[1]).astype(BF)
        v = dot(n, w_ref[2]).astype(BF)
        at = pl.ds(pl.multiple_of(base_row + ((t ^ r) & 1) * size, size), size)
        for h in range(heads):
            power = jnp.full((size, HD), (t * heads + h + 1).astype(F32) * (-8.0 / H), F32)
            hi, mid, lo = split3(jnp.exp2(power) * LOG2E * place)
            more = jnp.where(lane == 0, hi, jnp.where(lane == 1, mid, jnp.where(lane == 2, lo, base.astype(BF))))
            sl = slice(h * HD, (h + 1) * HD)
            q_ref[h, at, :HD] = q[:, sl]
            q_ref[h, at, HD:] = q_more
            k_ref[h, at, :HD] = k[:, sl]
            k_ref[h, at, HD:] = more
            v_ref[h, at, :HD] = v[:, sl]
            v_ref[h, at, HD:] = v_more


def attn_fwd_kernel(t_ref, q_ref, k_ref, v_ref, m0, m1, m2, m3, xa_ref, xb_ref, kept):
    heads, length, _ = q_ref.shape
    half = length // 8
    t = t_ref[0]
    row = lax.broadcasted_iota(jnp.int32, (half, half), 0)
    col = lax.broadcasted_iota(jnp.int32, (half, half), 1)
    keep = col <= row
    lane = lax.broadcasted_iota(jnp.int32, (half, HD), 1)
    for block in range(8):
        p, u = block // 2, block % 2
        start = block * half
        end = start + half
        for h in range(heads):
            q = q_ref[h, start:end, :]
            near = jnp.where(keep, dot(q, k_ref[h, start:end, :], NT), NEG)
            top = jnp.max(near, -1, keepdims=True)
            if start:
                far = dot(q, k_ref[h, :start, :], NT)
                top = jnp.maximum(top, jnp.max(far, -1, keepdims=True))
            out = dot(jnp.exp2(near - top).astype(BF), v_ref[h, start:end, :])
            if start:
                out = out + dot(jnp.exp2(far - top).astype(BF), v_ref[h, :start, :])
            total = out[:, HD : HD + 1]
            kept[p ^ t, u * half : (u + 1) * half, h * HD : (h + 1) * HD] = (out[:, :HD] / total).astype(BF)
            hi, mid, lo = split3(-(top + jnp.log2(total)))
            more = jnp.where(lane == 7, hi, jnp.where(lane == 8, mid, jnp.where(lane == 9, lo, q[:, HD:])))
            (xa_ref, xb_ref)[u][h, p] = more
    for r, out_ref in enumerate((m0, m1, m2, m3)):
        out_ref[...] = kept[r]


def attn_fwd(order, t, q, k, v):
    heads, length, _ = q.shape
    size = length // 4
    outs = [arr((size, heads * HD))] * 4 + [arr((heads, 4, size // 2, HD))] * 2
    scratch = [pltpu.VMEM((4, size, heads * HD), BF)]
    return order("attn_fwd", attn_fwd_kernel, outs, (t, q, k, v), limit=10, scratch=scratch, scalars=1)


def attn_bwd_kernel(u, t_ref, q_ref, k_ref, v_ref, x_ref, *rest):
    do_refs, o_refs, rest = rest[:4], rest[4:8], rest[8:]
    heads, length, _ = q_ref.shape
    half = length // 8
    pick = lambda ref, sl: ref[u * half : (u + 1) * half, sl]
    size = 2 * half
    width = heads * HD
    if u == 0:
        dq_ref, dk_ref, dv_ref, qs, ds, dqt = rest
    else:
        dq_first, dk_first, dv_first, g_ref, qs, ds, dqt = rest
    t = t_ref[0]
    lane = lax.broadcasted_iota(jnp.int32, (half, HD), 1)
    for h in range(heads):
        sl = slice(h * HD, (h + 1) * HD)
        for p in range(4):
            qs[h, p, :, :HD] = q_ref[h, (2 * p + u) * half : (2 * p + u + 1) * half, :HD]
            qs[h, p, :, HD:] = x_ref[h, p]
        for r in range(4):
            if r % 2:
                other = ((t & 1) ^ 1) * size + (half if r == 1 else 0)
                do = do_refs[r][pl.ds(pl.multiple_of(other, half), half), sl]
            else:
                do = do_refs[r][:half, sl]
            delta = jnp.sum(do.astype(F32) * pick(o_refs[r], sl).astype(F32), -1, keepdims=True)
            hi, mid, lo = split3(-delta)
            ds[h, r ^ t, :, :HD] = do
            ds[h, r ^ t, :, HD:] = jnp.where(
                lane == 0, hi, jnp.where(lane == 1, mid, jnp.where(lane == 2, lo, jnp.zeros_like(hi)))
            )
    near_rows = half * (1 + u)
    row = lax.broadcasted_iota(jnp.int32, (near_rows, half), 0)
    col = lax.broadcasted_iota(jnp.int32, (near_rows, half), 1)
    keep = row <= col + u * half
    for p in range(4):
        for h in range(heads):

            def part(rows, first, last, masked):
                at = slice(p * size, p * size + rows)
                n = (last - first) * half
                q = qs[h, first:last].reshape(n, 2 * HD)
                do = ds[h, first:last].reshape(n, 2 * HD)
                s = dot(k_ref[h, at, :], q, NT)
                if masked:
                    s = jnp.where(keep, s, NEG)
                e = jnp.exp2(s)
                de = (e * dot(v_ref[h, at, :], do, NT)).astype(BF)
                dv = dot(e.astype(BF), do[:, :HD])
                dk = dot(de, q[:, :HD])
                dq = dot(k_ref[h, at, :HD], de, TN)
                cols = slice(first * half, last * half)
                if p:
                    dqt[h, :, cols] += dq
                else:
                    dqt[h, :, cols] = dq
                return dk, dv

            dk, dv = part(near_rows, p, p + 1, True)
            if p < 3:
                dk_far, dv_far = part(size, p + 1, 4, False)
                if near_rows < size:
                    pad = jnp.zeros((size - near_rows, HD), F32)
                    dk, dv = jnp.concatenate([dk, pad]), jnp.concatenate([dv, pad])
                dk, dv = dk + dk_far, dv + dv_far
            elif near_rows < size:
                pad = jnp.zeros((size - near_rows, HD), F32)
                dk, dv = jnp.concatenate([dk, pad]), jnp.concatenate([dv, pad])
            dq = (dqt[h, :, p * half : (p + 1) * half].T * HD**-0.5).astype(BF)
            sl = slice(h * HD, (h + 1) * HD)
            if u == 0:
                dk_ref[h, p * size : (p + 1) * size] = dk
                dv_ref[h, p * size : (p + 1) * size] = dv
                dq_ref[p ^ t, :, sl] = dq
            else:
                at = slice(p * size, (p + 1) * size)
                g_ref[p ^ t, half:, sl] = dq
                g_ref[p ^ t, :, width + h * HD : width + (h + 1) * HD] = (
                    (dk + dk_first[h, at]) * (1.0 / LOG2E)
                ).astype(BF)
                g_ref[p ^ t, :, 2 * width + h * HD : 2 * width + (h + 1) * HD] = (dv + dv_first[h, at]).astype(BF)
    if u == 1:
        for r in range(4):
            g_ref[r, :half, :width] = dq_first[r]


def attn_bwd(order, u, t, q, k, v, x, do, o, first=()):
    heads, length, _ = q.shape
    half = length // 8
    width = heads * HD
    if u == 0:
        outs = [arr((4, half, width)), arr((heads, length, HD), F32), arr((heads, length, HD), F32)]
    else:
        outs = [arr((4, 2 * half, 3 * width))]
    return order(
        "attn_bwd",
        functools.partial(attn_bwd_kernel, u),
        outs,
        (t, q, k, v, x, *do, *o, *first),
        limit=16,
        scratch=[pltpu.VMEM((heads, 4, half, 2 * HD), BF)] * 2 + [pltpu.VMEM((heads, HD, 4 * half), F32)],
        scalars=1,
    )


def out_kernel(m0, m1, m2, m3, w0, w1, w2, w3, x_ref, bias_ref, gain_ref, shift_ref, resid_ref, n_ref, na_ref, nb_ref):
    half = na_ref.shape[0]
    for u, half_ref in enumerate((na_ref, nb_ref)):
        at = slice(u * half, (u + 1) * half)
        total = sum(dot(m[at], w[...]) for m, w in ((m0, w0), (m1, w1), (m2, w2), (m3, w3)))
        resid = x_ref[at, :].astype(F32) + (total + bias_ref[...])
        resid_ref[at] = resid
        hat, _ = standardized(resid)
        n = (hat * gain_ref[...] + shift_ref[...]).astype(BF)
        n_ref[at] = n
        half_ref[...] = n


def up_kernel(n0, n1, up_ref, act_ref, slope_ref):
    c = 0.7978845608028654
    rows = n0.shape[0]
    step = min(rows, 256)
    for i, n_ref in enumerate((n0, n1)):
        for first in range(0, rows, step):
            at = slice(i * rows + first, i * rows + first + step)
            v = dot(n_ref[first : first + step], up_ref[...])
            square = v * v
            th = jnp.tanh(v * (c + (c * 0.044715) * square))
            half_v = 0.5 * v
            act_ref[at] = (half_v + half_v * th).astype(BF)
            slope_ref[at] = (0.5 + 0.5 * th + half_v * (1.0 - th * th) * (c + (3 * c * 0.044715) * square)).astype(BF)


def back_kernel(u, g0, g1, slope_ref, up_ref, down_ref, dpre_ref, p0, *sends):
    rows = p0.shape[0]
    step = min(rows, 256)
    part = sends[0].shape[0]
    for i, g_ref in enumerate((g0, g1)):
        for first in range(0, rows, step):
            at = slice(i * rows + first, i * rows + first + step)
            g = g_ref[u * rows + first : u * rows + first + step]
            dpre = (dot(g, down_ref[...], NT) * slope_ref[at].astype(F32)).astype(BF)
            dpre_ref[at] = dpre
            total = dot(dpre, up_ref[...], NT).astype(BF)
            if i == 0:
                p0[first : first + step] = total
            elif part < step:
                for n, out_ref in enumerate(sends):
                    out_ref[...] = total[n * part : (n + 1) * part]
            else:
                sends[0][first : first + step] = total


def down_kernel(sources, *refs):
    count = max(i for i, _ in sources) + 1
    acts, w_ref, outs = refs[:count], refs[count], refs[count + 1 :]
    half = outs[0].shape[0] // 2
    rows = outs[1].shape[0]
    for n, (i, first) in enumerate(sources):
        out = dot(acts[i][first : first + half], w_ref[...]).astype(BF)
        if n < 2:
            outs[0][n * half : (n + 1) * half] = out
        elif rows > half:
            outs[1][(n - 2) * half : (n - 1) * half] = out
        else:
            for m in range(half // rows):
                outs[1 + (n - 2) * (half // rows) + m][...] = out[m * rows : (m + 1) * rows]


def mid_kernel(
    u, p0, c1, y2, resid_ref, cot_ref, seg_ref, gain_ref, w0, w1, w2, w3, dresid_ref, dattn_ref, m0, m1, m23, sums_ref
):
    half = y2.shape[0]
    sl = slice(u * half, (u + 1) * half)
    grad = p0[sl].astype(F32) + c1[sl].astype(F32) + y2[...].astype(F32)
    hat, inverse = standardized(resid_ref[sl])
    g = jnp.where(seg_ref[sl] != 0, cot_ref[sl].astype(F32), 0.0)
    dresid = g + norm_back(grad, gain_ref[...], hat, inverse)
    dresid_ref[...] = dresid
    dattn = dresid.astype(BF)
    dattn_ref[...] = dattn
    m0[...] = dot(dattn, w0[...], NT).astype(BF)
    m1[...] = dot(dattn, w1[...], NT).astype(BF)
    m23[:half] = dot(dattn, w2[...], NT).astype(BF)
    m23[half:] = dot(dattn, w3[...], NT).astype(BF)
    rows = [grad * hat, grad, dresid, g]
    sums_ref[...] = jnp.concatenate([jnp.sum(v, 0, keepdims=True) for v in rows] + [jnp.zeros((4, hat.shape[1]), F32)])


def pass_kernel(far_ref, own_ref, out_ref):
    half = own_ref.shape[0]
    out_ref[:half] = far_ref[half:]
    out_ref[half:] = own_ref[...]


def dn1_kernel(pair, g_ref, w_ref, a_ref, *sends):
    width = w_ref.shape[2]
    product = lambda r, at: sum(dot(g_ref[r, at, c * width : (c + 1) * width], w_ref[c], NT) for c in range(3)).astype(BF)
    rows = sends[0].shape[0]
    for i, out_ref in enumerate(sends):
        out_ref[...] = product(2 * pair + 1, slice(i * rows, (i + 1) * rows))
    a_ref[...] = product(2 * pair, slice(0, a_ref.shape[0]))


def last_kernel(p0, c1, y2, x_ref, da, db, gain_ref, out_ref):
    grad = p0[...].astype(F32) + c1[...].astype(F32) + y2[...].astype(F32)
    hat, inverse = standardized(x_ref[...].astype(F32))
    dresid = jnp.where(pl.program_id(0) < 2, da[...], db[...])
    out_ref[...] = dresid + norm_back(grad, gain_ref[...], hat, inverse)


def result_kernel(resid_ref, p0, c1, y2, seg_ref, bias_ref, out_ref):
    total = p0[...].astype(F32) + c1[...].astype(F32) + y2[...].astype(F32)
    out_ref[...] = jnp.where(seg_ref[...] != 0, resid_ref[...] + total + bias_ref[...], 0.0).astype(BF)


def quarters(kinds, size, width):
    rows = size // 4
    maps = {
        "w": lambda i: (i, 0),
        "a": lambda i: (jnp.minimum(i, 1), 0),
        "b": lambda i: (jnp.maximum(i - 2, 0), 0),
        "r": lambda i: (0, 0),
        "s": lambda i: (i, 0),
    }
    specs = [pl.BlockSpec((1 if k == "r" else rows, 1 if k == "s" else width), maps[k]) for k in kinds]
    return specs[:-1], (specs[-1],), (4,)


def order_of(bits):
    rest = [0]
    for bit in reversed(bits[1:]):
        rest = [e | (1 << bit) for e in rest] + rest
    return [e | (1 << bits[0]) for e in rest], rest


def ffn_grad_kernel(bits, tile, count, pairs, d_ref, *refs):
    lefts, rights, outs = refs[:count], refs[count:], refs[-2:]
    single = refs[-1].dtype == F32
    for out_ref, blocks in zip(outs, ([], list(range(8))) if single else order_of(bits)):
        for i, e in enumerate(blocks):
            cols = pl.ds(bits_of(d_ref[0], e, tile), tile)
            total = refs[-3][e] if refs[-3].dtype == F32 else 0.0
            for left, first, rows, right, at in pairs:
                total += dot(lefts[left][first : first + rows, cols], rights[right][at : at + rows], TN)
            out_ref[i] = total.astype(out_ref.dtype)


def ffn_grad(order, name, bits, d, lefts, rights, pairs, so_far=(), more=False):
    tile = lefts[0].shape[1] // 8
    body = functools.partial(ffn_grad_kernel, bits, tile, len(lefts), pairs)
    shape = (tile, rights[0].shape[1])
    outs = [arr((8, *shape), F32)] if more else [arr((4, *shape))] * 2
    return order(name, body, outs, (d, *lefts, *rights, *so_far), scalars=1)


def out_grad_kernel(tile, d_ref, la, lb, m0, m1, m2, m3, send_ref, keep_ref):
    half, width = la.shape[0], m0.shape[1]
    for e in range(8):
        cols = pl.ds(bits_of(d_ref[0], e, tile), tile)
        for r, m in enumerate((m0, m1, m2, m3)):
            total = (dot(la[:, cols], m[:half], TN) + dot(lb[:, cols], m[half:], TN)).astype(BF)
            out_ref = send_ref if r % 2 else keep_ref
            out_ref[e, :, (r // 2) * width : (r // 2 + 1) * width] = total


def qkv_grad_kernel(orders, tile, d_ref, n0, n1, n2, n3, g_ref, w_ref, sums_a, sums_b, gain_ref, shift_ref, keep_ref, got_ref, *refs):
    outs, kept, lines = refs[:4], refs[4], refs[5]
    width = w_ref.shape[2]
    size = g_ref.shape[1]
    count = jnp.ones((8, size), BF)
    weighted, shifted = 0.0, 0.0
    for c in range(3):
        sl = slice(c * width, (c + 1) * width)
        total = sum(dot(n[:size, :], g_ref[r, :, sl], TN) for r, n in enumerate((n0, n1, n2, n3)))
        for s in range(8):
            kept[s ^ d_ref[0], :, sl] = total[s * tile : (s + 1) * tile].astype(BF)
        w = w_ref[c].astype(F32)
        weighted += total * w
        shifted += sum(dot(count, g_ref[r, :, sl]) for r in range(4))[:1] * w
    ones = jnp.ones((8, width), F32)
    high = lambda v: lax.dot_general(ones, v, NT, precision=lax.Precision.HIGHEST, preferred_element_type=F32)
    shift_sum = high(shifted)[:1]
    gain_sum = (high(weighted)[:1] - shift_ref[...] * shift_sum) / gain_ref[...]
    both = sums_a[...] + sums_b[...]
    rows = jnp.concatenate([gain_sum, shift_sum, both[:4], jnp.zeros((10, both.shape[1]), F32)]).astype(BF)
    for s in range(8):
        lines[s ^ d_ref[0]] = rows[:, s * tile : (s + 1) * tile]
    for e in range(8):
        kept[e, :, 3 * width :] = (keep_ref[e].astype(F32) + got_ref[e].astype(F32)).astype(BF)
    part = outs[0].shape[2]
    for m, bits in enumerate(orders):
        for k, blocks in enumerate(order_of(bits)):
            for i, e in enumerate(blocks):
                outs[2 * m + k][i, :tile] = kept[e, :, m * part : (m + 1) * part]
                outs[2 * m + k][i, tile:] = jnp.zeros((16, part), BF)
                if m == 0:
                    outs[k][i, tile:, :tile] = lines[e]


def add_kernel(*refs):
    first, others, out_ref = refs[0], refs[1:-1], refs[-1]
    at = 0
    for ref in others:
        rows = ref.shape[0]
        out_ref[at : at + rows] = (first[at : at + rows].astype(F32) + ref[...].astype(F32)).astype(BF)
        at += rows


def add_pair_kernel(t_ref, *refs):
    first, others, out_ref = refs[0], refs[1:-1], refs[-1]
    rows = others[0].shape[0] // 2
    theirs = pl.ds(pl.multiple_of(((t_ref[0] & 1) ^ 1) * rows, rows), rows)
    for i, ref in enumerate(others):
        at = slice(i * rows, (i + 1) * rows)
        out_ref[at] = (first[at].astype(F32) + ref[theirs].astype(F32)).astype(BF)


def stage_kernel(turned, groups, later, *refs):
    count = len(turned)
    own, got, outs = refs[:count], refs[count : count + len(groups)], refs[count + len(groups) :]
    total = [None] * count
    for ref, group in zip(got, groups):
        at = 0
        for m in group:
            width = own[m].shape[2]
            total[m] = own[m][...].astype(F32) + ref[:, :, at : at + width].astype(F32)
            at += width
    if not later:
        for m in range(count):
            outs[m][...] = total[m][0].T if turned[m] else total[m][0]
        return
    for ref, group in zip(outs[count:], later):
        at = 0
        for m in group:
            blocks, _, width = total[m].shape
            outs[m][...] = total[m][blocks // 2 :].astype(BF)
            ref[:, :, at : at + width] = total[m][: blocks // 2].astype(BF)
            at += width


def after(x, *others):
    return lax.optimization_barrier((x, *others))[0]


def to_core(x):
    return lax.ppermute(x, "tensor", [(i, i ^ 1) for i in range(4)])


def to_chip(x):
    return lax.ppermute(x, "tensor", [(i, i ^ 2) for i in range(4)])


def to_diag(x):
    return lax.ppermute(x, "tensor", [(i, i ^ 3) for i in range(4)])


def gather(x):
    far = to_chip(x)
    return [x, to_core(x), far, to_core(far)]


def pair_gather(x):
    return lax.all_gather(x, "tensor", axis=0, tiled=True, axis_index_groups=[[0, 1], [2, 3]])


class Reduce:
    def __init__(self, order, dp, d, *matrices):
        self.order, self.dp, self.d = order, dp, d
        self.low = dp.bit_length() - 4
        self.own = [parts[1] for parts, _, _ in matrices]
        self.bits = [list(bits[1:]) for _, bits, _ in matrices]
        self.turned = [turned for _, _, turned in matrices]
        self.groups = [[m] for m in range(len(matrices))]
        self.got = [self.swap(parts[0], bits[0]) for parts, bits, _ in matrices]

    def merge(self, other):
        count = len(self.own)
        self.own, self.bits, self.turned = self.own + other.own, self.bits + other.bits, self.turned + other.turned
        self.groups, self.got = self.groups + [[m + count for m in g] for g in other.groups], self.got + other.got

    def take(self, m):
        other = Reduce(self.order, self.dp, self.d)
        g = self.groups.index([m])
        other.own, other.bits, other.turned = [self.own.pop(m)], [self.bits.pop(m)], [self.turned.pop(m)]
        other.groups, other.got = [[0]], [self.got.pop(g)]
        self.groups.pop(g)
        return other

    def swap(self, x, bit):
        return lax.ppermute(x, "dp", [(i, i ^ (1 << (bit + self.low))) for i in range(self.dp)])

    def stage(self):
        count = len(self.own)
        turned = [bool(f) and not self.low for f in self.turned]
        later = []
        if any(self.bits):
            for key in sorted({(self.bits[m][0], self.own[m].shape[:2]) for m in range(count)}):
                later.append([m for m in range(count) if (self.bits[m][0], self.own[m].shape[:2]) == key])
            outs = [arr((own.shape[0] // 2, *own.shape[1:])) for own in self.own]
            for group in later:
                blocks, rows, _ = outs[group[0]].shape
                outs.append(arr((blocks, rows, sum(self.own[m].shape[2] for m in group))))
        else:
            shapes = [own.shape for own in self.own]
            outs = [arr((s[2], s[1]) if f else s[1:], F32) for s, f in zip(shapes, turned)]
        body = functools.partial(stage_kernel, turned, self.groups, later)
        sums = self.order("stage", body, outs, (*self.own, *self.got))
        if not later:
            return [s if f is None else self.rest(s, f) for s, f in zip(sums, self.turned)]
        self.own = list(sums[:count])
        self.got = [self.swap(x, self.bits[group[0]][0]) for x, group in zip(sums[count:], later)]
        self.groups, self.bits = later, [bits[1:] for bits in self.bits]
        return None

    def rest(self, total, turned):
        for bit in range(self.low - 1, -1, -1):
            mine = (self.d >> bit) & 1
            view = total.reshape(2, total.shape[0] // 2, total.shape[1])
            send = lax.dynamic_index_in_dim(view, 1 - mine, 0, keepdims=False)
            keep = lax.dynamic_index_in_dim(view, mine, 0, keepdims=False)
            total = keep + lax.ppermute(send, "dp", [(i, i ^ (1 << bit)) for i in range(self.dp)])
        return total.T if turned and self.low else total


def place_kernel(rows, d_ref, in_ref, out_ref):
    for i in range(8):
        e = (i & 1) << 2 | (i & 2) | i >> 2
        out_ref[pl.ds(bits_of(d_ref[0], e, rows), rows)] = in_ref[i * rows : (i + 1) * rows]


def local(dp, block_input, segment_ids, w_qkv, w_out, w_up, w_down, ln1_gain, ln1_bias, ln2_gain, ln2_bias, out_bias, down_bias, cotangent):
    size, width = block_input.shape[1:]
    half = size // 2
    hidden = w_up.shape[1]
    local_width = w_qkv.shape[2]
    heads = local_width // HD
    t = lax.axis_index("tensor")
    d = lax.axis_index("dp")
    low = dp.bit_length() - 4
    t_arg = t[None].astype(jnp.int32)
    block_arg = (d >> low)[None].astype(jnp.int32)
    x = block_input[0]
    cot = cotangent[0]
    seg = segment_ids[0][:, None]
    gain1, shift1, gain2, shift2 = ln1_gain[None], ln1_bias[None], ln2_gain[None], ln2_bias[None]
    token = (size, width)
    chunk = (half, width)
    order = Order()

    part = local_width // 8
    wo_part = to_chip(lax.dynamic_slice_in_dim(w_out, (d >> low) * part, part, 0))
    (n1_own,) = order("norm", norm_kernel, [arr((size + 16, width))], (x, segment_ids, gain1, shift1))
    n1_far, n1_core = to_chip(after(n1_own, wo_part)), to_core(n1_own)

    def spread(x, bit):
        sent = lax.ppermute(x, "dp", [(i, i ^ (1 << (bit + low))) for i in range(dp)])
        return jnp.concatenate([x, sent])

    wo_part = spread(order.then(wo_part), 2)
    half_row = [arr((heads, 2 * size, 2 * HD))] * 3
    near = order("qkv", functools.partial(qkv_kernel, 0, heads), half_row, (t_arg, n1_own, n1_core, w_qkv), scalars=1)
    (dffn_own,) = order("masks", masks_kernel, [arr(token)], (cot, seg))
    dffn_core = to_core(dffn_own)
    wo_part = spread(spread(order.then(wo_part), 1), 0)
    body = functools.partial(place_kernel, part)
    (wo_far,) = order("place", body, [arr(w_out.shape)], (block_arg, wo_part), scalars=1)
    wo = [w_out, to_core(order.then(w_out)), wo_far, to_core(wo_far)]
    n1 = [n1_own, n1_core, n1_far, to_core(order.then(n1_far))]
    dffn_far = to_chip(after(dffn_own, n1_far))
    order.wait(wo[1], wo[3])
    args = (t_arg, n1[2], n1[3], w_qkv, *near)
    row = [arr((heads, 4 * size, 2 * HD))] * 3
    q, k, v = order("qkv", functools.partial(qkv_kernel, 2, heads), row, args, scalars=1)

    *o, x_a, x_b = attn_fwd(order, t_arg, q, k, v)
    mixed = [o[0], to_core(o[1]), to_chip(o[2]), to_diag(o[3])]
    args = (*mixed, *wo, x, out_bias[None], gain2, shift2)
    resid, n2_own, n2_a, n2_b = order("out_proj", out_kernel, [arr(token, F32), arr(token)] + [arr(chunk)] * 2, args)
    n2_a = to_chip(n2_a)
    n2_core = to_core(n2_own)
    n2_b = to_chip(n2_b)
    dffn = [dffn_own, dffn_core, dffn_far, to_core(order.then(dffn_far))]
    order.wait(dffn[3])

    def up(first, second):
        outs = [arr((2 * first.shape[0], hidden))] * 2
        return order("up", up_kernel, outs, (first, second, w_up))

    def back(u, grads, slope):
        rows = slope.shape[0] // 2
        sends = [arr((rows, width))] if rows == size else [arr((rows // 2, width))] * 2
        outs = [arr(slope.shape), arr((rows, width)), *sends]
        return order("back", functools.partial(back_kernel, u), outs, (*grads, slope, w_up, w_down))

    act_near, slope = up(n2_own, n2_core)
    dpre_near, p0, p1 = back(0, dffn[:2], slope)
    p1 = to_core(p1)
    body = functools.partial(down_kernel, [(0, i * half) for i in range(4)])
    ffn0, ffn1 = order("down", body, [arr(token)] * 2, (act_near, w_down))
    n2_a = [n2_a, to_core(order.then(n2_a))]
    order.wait(p1)
    ffn1 = to_core(ffn1)
    act_a, slope = up(*n2_a)
    dpre_a, p2, *send = back(0, dffn[2:], slope)
    send = [to_core(x) for x in send]
    (chip,) = order("add", add_kernel, [arr(chunk)], (p2, *send))
    chip_a = to_chip(chip)
    bits = ((0, 1, 2), (1, 0, 2))
    pairs = [(0, 0, size, 0, 0), (1, 0, size, 0, size), (2, 0, half, 1, 0), (3, 0, half, 1, half)]
    lefts = [n2_own, n2_core, *n2_a]
    so_far = ffn_grad(order, "up_grad", bits[0], block_arg, lefts, [dpre_near, dpre_a], pairs, more=True)
    n2_b = [n2_b, to_core(order.then(n2_b))]
    act_b, slope = up(*n2_b)
    dpre_b, p2, *send = back(1, dffn[2:], slope)
    send = [pair_gather(x) for x in send]
    (chip,) = order("add", add_pair_kernel, [arr(chunk)], (t_arg, p2, *send), scalars=1)
    chip_b = to_chip(chip)
    order.wait(ffn1)


    def middle(u, y2):
        piece = (half, local_width)
        outs = [arr(chunk, F32), arr(chunk), arr(piece), arr(piece), arr((size, local_width)), arr((8, width), F32)]
        args = (p0, p1, y2, resid, cot, seg, gain2, *wo)
        return order("mid", functools.partial(mid_kernel, u), outs, args)

    def arrived(far, m0, m1):
        (send,) = order("pass", pass_kernel, [arr((size, local_width))], (far, m1))
        got = pair_gather(send)
        return m0, got, far, got

    dresid_a, dattn_a, m0a, m1a, send_a, sums_a = middle(0, chip_a)
    far_a = to_chip(send_a)
    pairs = [(i, 0, half, 0, i * half) for i in range(2)]
    parts = ffn_grad(order, "up_grad", bits[0], block_arg, n2_b, [dpre_b], pairs, so_far)
    up_reduce = Reduce(order, dp, d, (parts, bits[0], False))
    pairs = [(0, 0, size, 0, 0), (1, 0, size, 0, size)]
    pairs += [(2 + i, u * half, half, 1 + u, i * half) for u in range(2) for i in range(2)]
    parts = ffn_grad(order, "down_grad", bits[1], block_arg, dffn, [act_near, act_a, act_b], pairs)
    down_reduce = Reduce(order, dp, d, (parts, bits[1], True))
    dresid_b, dattn_b, m0b, m1b, send_b, sums_b = middle(1, chip_b)
    far_b = to_chip(send_b)

    do = arrived(far_a, m0a, m1a)
    tile = width // 8
    outs = [arr((8, tile, 2 * local_width))] * 2
    args = (block_arg, dattn_a, dattn_b, *mixed)
    out_send, out_keep = order("out_grad", functools.partial(out_grad_kernel, tile), outs, args, scalars=1)
    out_send = to_core(out_send)
    order.wait(far_b)
    first = attn_bwd(order, 0, t_arg, q, k, v, x_a, do, o)
    do = arrived(far_b, m0b, m1b)
    (dqkv,) = attn_bwd(order, 1, t_arg, q, k, v, x_b, do, o, first)
    own, *send = order("dn1", functools.partial(dn1_kernel, 1), [arr(token)] + [arr(chunk)] * 2, (dqkv, w_qkv))
    send = [to_core(x) for x in send]
    up_reduce.stage()
    down_reduce.stage()
    (chip,) = order("add", add_kernel, [arr(token)], (own, *send))
    dn1_chip = to_chip(chip)
    dn1_own, dn1_core = order("dn1", functools.partial(dn1_kernel, 0), [arr(token)] * 2, (dqkv, w_qkv))
    dn1_core = to_core(dn1_core)
    cols = 5 * local_width // 2
    outs = [arr((4, tile + 16, cols))] * 4
    args = (block_arg, *n1, dqkv, w_qkv, sums_a, sums_b, gain1, shift1, out_keep, out_send)
    scratch = [pltpu.VMEM((8, tile, 2 * cols), BF), pltpu.VMEM((8, 16, tile), BF)]
    body = functools.partial(qkv_grad_kernel, bits, tile)
    parts = order("qkv_grad", body, outs, args, scratch=scratch, scalars=1)
    up_reduce.merge(down_reduce)
    up_reduce.stage()
    parts = [order.then(parts[0]), parts[1], order.then(parts[2]), parts[3]]
    qkv_reduce = Reduce(order, dp, d, (parts[:2], bits[0], None), (parts[2:], bits[1], None))
    blocks = quarters("wwwwabrw", *token)
    args = (dn1_own, dn1_core, dn1_chip, x, dresid_a, dresid_b, gain1)
    (x_grad,) = order("last", last_kernel, [arr(token, F32)], args, blocks=blocks)
    body = functools.partial(down_kernel, [(0, 0), (1, 0), (0, half), (1, half)])
    ffn2, *send = order("down", body, [arr(token)] + [arr((size // 4, width))] * 4, (act_a, act_b, w_down))
    send = [pair_gather(x) for x in send]
    order.wait(*send)
    up_sum, down_sum = up_reduce.stage()
    (ffn_chip,) = order("add", add_pair_kernel, [arr(token)], (t_arg, ffn2, *send), scalars=1)
    ffn_chip = to_chip(ffn_chip)
    qkv_reduce.stage()
    qkv_reduce.stage()
    args = (resid, ffn0, ffn1, ffn_chip, seg, down_bias[None])
    (output,) = order("result", result_kernel, [arr(token)], args, blocks=quarters("wwwwsrw", *token))
    first, second = qkv_reduce.stage()
    lines = qkv_reduce.rest(first[tile : tile + 6, :tile].T, False)
    lines = lines + to_core(lines) + to_chip(lines) + to_diag(lines)
    chunk = width // dp // 4
    vectors = lax.dynamic_slice_in_dim(lines, t * chunk, chunk, 0)
    both = jnp.concatenate([qkv_reduce.rest(p[:tile], False) for p in (first, second)], 1)
    qkv_sum = both[:, : 3 * local_width].reshape(width // dp, 3, local_width).transpose(1, 0, 2)
    out_sum = both[:, 3 * local_width : 4 * local_width] + to_chip(both[:, 4 * local_width :])
    return (output[None], x_grad[None], qkv_sum, out_sum.T, up_sum, down_sum, *(vectors[:, i] for i in range(6)))


def solution(mesh):
    row = P("dp", "tensor", None)
    matrix = (P(None, None, "tensor"), P("tensor", None), P(None, "tensor"), P("tensor", None))
    in_specs = (row, P("dp", "tensor"), *matrix) + (P(),) * 6 + (row,)
    vector = P(("dp", "tensor"))
    out_specs = (row, row, P(None, "dp", "tensor"), P("tensor", "dp"), P("dp", "tensor"), P("tensor", "dp")) + (vector,) * 6
    run = functools.partial(local, mesh.shape["dp"])
    return jax.shard_map(run, mesh=mesh, in_specs=in_specs, out_specs=out_specs, check_vma=False)
```

```python
import functools

import jax
import jax.numpy as jnp
from jax import lax
from jax.experimental import pallas as pl
from jax.experimental.pallas import tpu as pltpu
from jax.sharding import PartitionSpec as P

H = 8
HD = 128
EPS = 1e-05
NEG = -1e30
LOG2E = 1.4426950408889634
BF = jnp.bfloat16
F32 = jnp.float32
NN = (((1,), (0,)), ((), ()))
NT = (((1,), (1,)), ((), ()))
TN = (((0,), (0,)), ((), ()))
VMEM = pl.BlockSpec(memory_space=pltpu.VMEM)
SMEM = pl.BlockSpec(memory_space=pltpu.SMEM)


def dot(a, b, dims=NN):
    return lax.dot_general(a, b, dims, preferred_element_type=F32)


def call(name, body, outs, args, limit=12, scratch=(), scalars=0, blocks=None):
    in_specs, out_specs, grid = blocks or ([SMEM] * scalars + [VMEM] * (len(args) - scalars), (VMEM,) * len(outs), ())
    return pl.pallas_call(
        body,
        out_shape=tuple(outs),
        grid=grid,
        in_specs=in_specs,
        out_specs=out_specs,
        scratch_shapes=list(scratch),
        name=name,
        cost_estimate=pl.CostEstimate(flops=1, bytes_accessed=1, transcendentals=0),
        compiler_params=pltpu.CompilerParams(vmem_limit_bytes=limit * 2**20),
    )(*args)


def arr(shape, dtype=BF):
    return jax.ShapeDtypeStruct(shape, dtype)


def split3(v):
    hi = v.astype(BF)
    rest = v - hi.astype(F32)
    mid = rest.astype(BF)
    return hi, mid, (rest - mid.astype(F32)).astype(BF)


def standardized(values):
    center = values - jnp.mean(values, -1, keepdims=True)
    inverse = lax.rsqrt(jnp.mean(center * center, -1, keepdims=True) + EPS)
    return center * inverse, inverse


def norm_back(grad, gain, hat, inverse):
    e = grad * gain
    return (e - jnp.mean(e, -1, keepdims=True) - hat * jnp.mean(e * hat, -1, keepdims=True)) * inverse


def bits_of(index, place, value):
    return pl.multiple_of((index ^ place) * value, value)


class Order:
    def __init__(self):
        self.last = ()

    def __call__(self, name, body, outs, args, limit=12, scratch=(), scalars=0, blocks=None):
        args = list(args)
        if self.last:
            args[scalars] = after(args[scalars], *self.last)
        got = call(name, body, outs, args, limit, scratch, scalars, blocks)
        self.last = (got[-1],)
        return got

    def then(self, x):
        return after(x, *self.last)

    def wait(self, *values):
        self.last += values


def norm_kernel(x_ref, seg_ref, gain_ref, shift_ref, out_ref):
    size, width = x_ref.shape
    hat, _ = standardized(x_ref[...].astype(F32))
    out_ref[:size] = (hat * gain_ref[...] + shift_ref[...]).astype(BF)
    ids = jnp.broadcast_to(seg_ref[...].astype(F32), (16, size)).astype(BF)
    out_ref[size:, :size] = ids
    out_ref[size:, size:] = jnp.zeros((16, width - size), BF)


def masks_kernel(cot_ref, seg_ref, out_ref):
    out_ref[...] = jnp.where(seg_ref[...] != 0, cot_ref[...], jnp.zeros((), BF))


def qkv_kernel(r0, heads, t_ref, n0, n1, w_ref, *refs):
    size = n0.shape[0] - 16
    t = t_ref[0]
    q_ref, k_ref, v_ref = refs[-3:]
    base_row = 0
    if len(refs) > 3:
        mine = pl.ds(pl.multiple_of((t >> 1) * (2 * size), size), 2 * size)
        for given, out_ref in zip(refs[:3], refs[3:]):
            out_ref[:, mine, :] = given[...]
        base_row = ((t >> 1) ^ 1) * (2 * size)
    lane = lax.broadcasted_iota(jnp.int32, (size, HD), 1)
    row = lax.broadcasted_iota(jnp.int32, (size, HD), 0)
    article = (lane >= 3) & (lane < 7)
    v_more = jnp.where(lane < 3, 1.0, 0.0).astype(BF)
    for r, n_ref in ((r0, n0), (r0 + 1, n1)):
        n = n_ref[:size]
        place = ((t ^ r) * size + row).astype(F32)
        ids = jnp.broadcast_to(n_ref[size:, :size].astype(F32)[:1], (HD, size)).T
        hot = ids == (lane - 3).astype(F32)
        q_more = jnp.where((lane < 3) | (article & hot), 1.0, 0.0).astype(BF)
        base = jnp.where(article, jnp.where(hot, 0.0, NEG), jnp.where((lane >= 7) & (lane < 10), 1.0, 0.0))
        q = (dot(n, w_ref[0]) * (HD**-0.5 * LOG2E)).astype(BF)
        k = dot(n, w_ref[1]).astype(BF)
        v = dot(n, w_ref[2]).astype(BF)
        at = pl.ds(pl.multiple_of(base_row + ((t ^ r) & 1) * size, size), size)
        for h in range(heads):
            power = jnp.full((size, HD), (t * heads + h + 1).astype(F32) * (-8.0 / H), F32)
            hi, mid, lo = split3(jnp.exp2(power) * LOG2E * place)
            more = jnp.where(lane == 0, hi, jnp.where(lane == 1, mid, jnp.where(lane == 2, lo, base.astype(BF))))
            sl = slice(h * HD, (h + 1) * HD)
            q_ref[h, at, :HD] = q[:, sl]
            q_ref[h, at, HD:] = q_more
            k_ref[h, at, :HD] = k[:, sl]
            k_ref[h, at, HD:] = more
            v_ref[h, at, :HD] = v[:, sl]
            v_ref[h, at, HD:] = v_more


def attn_fwd_kernel(t_ref, q_ref, k_ref, v_ref, m0, m1, m2, m3, xa_ref, xb_ref, kept):
    heads, length, _ = q_ref.shape
    half = length // 8
    t = t_ref[0]
    row = lax.broadcasted_iota(jnp.int32, (half, half), 0)
    col = lax.broadcasted_iota(jnp.int32, (half, half), 1)
    keep = col <= row
    lane = lax.broadcasted_iota(jnp.int32, (half, HD), 1)
    for block in range(8):
        p, u = block // 2, block % 2
        start = block * half
        end = start + half
        for h in range(heads):
            q = q_ref[h, start:end, :]
            near = jnp.where(keep, dot(q, k_ref[h, start:end, :], NT), NEG)
            top = jnp.max(near, -1, keepdims=True)
            if start:
                far = dot(q, k_ref[h, :start, :], NT)
                top = jnp.maximum(top, jnp.max(far, -1, keepdims=True))
            out = dot(jnp.exp2(near - top).astype(BF), v_ref[h, start:end, :])
            if start:
                out = out + dot(jnp.exp2(far - top).astype(BF), v_ref[h, :start, :])
            total = out[:, HD : HD + 1]
            kept[p ^ t, u * half : (u + 1) * half, h * HD : (h + 1) * HD] = (out[:, :HD] / total).astype(BF)
            hi, mid, lo = split3(-(top + jnp.log2(total)))
            more = jnp.where(lane == 7, hi, jnp.where(lane == 8, mid, jnp.where(lane == 9, lo, q[:, HD:])))
            (xa_ref, xb_ref)[u][h, p] = more
    for r, out_ref in enumerate((m0, m1, m2, m3)):
        out_ref[...] = kept[r]


def attn_fwd(order, t, q, k, v):
    heads, length, _ = q.shape
    size = length // 4
    outs = [arr((size, heads * HD))] * 4 + [arr((heads, 4, size // 2, HD))] * 2
    scratch = [pltpu.VMEM((4, size, heads * HD), BF)]
    return order("attn_fwd", attn_fwd_kernel, outs, (t, q, k, v), limit=10, scratch=scratch, scalars=1)


def attn_bwd_kernel(u, t_ref, q_ref, k_ref, v_ref, x_ref, *rest):
    do_refs, o_refs, rest = rest[:4], rest[4:8], rest[8:]
    heads, length, _ = q_ref.shape
    half = length // 8
    pick = lambda ref, sl: ref[u * half : (u + 1) * half, sl]
    size = 2 * half
    width = heads * HD
    if u == 0:
        dq_ref, dk_ref, dv_ref, qs, ds, dqt = rest
    else:
        dq_first, dk_first, dv_first, g_ref, qs, ds, dqt = rest
    t = t_ref[0]
    lane = lax.broadcasted_iota(jnp.int32, (half, HD), 1)
    for h in range(heads):
        sl = slice(h * HD, (h + 1) * HD)
        for p in range(4):
            qs[h, p, :, :HD] = q_ref[h, (2 * p + u) * half : (2 * p + u + 1) * half, :HD]
            qs[h, p, :, HD:] = x_ref[h, p]
        for r in range(4):
            if r % 2:
                other = (((t & 1) ^ 1) * size if u == 0 else 0) + (half if r == 1 else 0)
                do = do_refs[r][pl.ds(pl.multiple_of(other, half), half), sl]
            else:
                do = do_refs[r][:half, sl]
            delta = jnp.sum(do.astype(F32) * pick(o_refs[r], sl).astype(F32), -1, keepdims=True)
            hi, mid, lo = split3(-delta)
            ds[h, r ^ t, :, :HD] = do
            ds[h, r ^ t, :, HD:] = jnp.where(
                lane == 0, hi, jnp.where(lane == 1, mid, jnp.where(lane == 2, lo, jnp.zeros_like(hi)))
            )
    near_rows = half * (1 + u)
    row = lax.broadcasted_iota(jnp.int32, (near_rows, half), 0)
    col = lax.broadcasted_iota(jnp.int32, (near_rows, half), 1)
    keep = row <= col + u * half
    for p in range(4):
        for h in range(heads):

            def part(rows, first, last, masked):
                at = slice(p * size, p * size + rows)
                n = (last - first) * half
                q = qs[h, first:last].reshape(n, 2 * HD)
                do = ds[h, first:last].reshape(n, 2 * HD)
                s = dot(k_ref[h, at, :], q, NT)
                if masked:
                    s = jnp.where(keep, s, NEG)
                e = jnp.exp2(s)
                de = (e * dot(v_ref[h, at, :], do, NT)).astype(BF)
                dv = dot(e.astype(BF), do[:, :HD])
                dk = dot(de, q[:, :HD])
                dq = dot(k_ref[h, at, :HD], de, TN)
                cols = slice(first * half, last * half)
                if p:
                    dqt[h, :, cols] += dq
                else:
                    dqt[h, :, cols] = dq
                return dk, dv

            dk, dv = part(near_rows, p, p + 1, True)
            if p < 3:
                dk_far, dv_far = part(size, p + 1, 4, False)
                if near_rows < size:
                    pad = jnp.zeros((size - near_rows, HD), F32)
                    dk, dv = jnp.concatenate([dk, pad]), jnp.concatenate([dv, pad])
                dk, dv = dk + dk_far, dv + dv_far
            elif near_rows < size:
                pad = jnp.zeros((size - near_rows, HD), F32)
                dk, dv = jnp.concatenate([dk, pad]), jnp.concatenate([dv, pad])
            dq = (dqt[h, :, p * half : (p + 1) * half].T * HD**-0.5).astype(BF)
            sl = slice(h * HD, (h + 1) * HD)
            if u == 0:
                dk_ref[h, p * size : (p + 1) * size] = dk
                dv_ref[h, p * size : (p + 1) * size] = dv
                dq_ref[p ^ t, :, sl] = dq
            else:
                at = slice(p * size, (p + 1) * size)
                g_ref[p ^ t, half:, sl] = dq
                g_ref[p ^ t, :, width + h * HD : width + (h + 1) * HD] = (
                    (dk + dk_first[h, at]) * (1.0 / LOG2E)
                ).astype(BF)
                g_ref[p ^ t, :, 2 * width + h * HD : 2 * width + (h + 1) * HD] = (dv + dv_first[h, at]).astype(BF)
    if u == 1:
        for r in range(4):
            g_ref[r, :half, :width] = dq_first[r]


def attn_bwd(order, u, t, q, k, v, x, do, o, first=()):
    heads, length, _ = q.shape
    half = length // 8
    width = heads * HD
    if u == 0:
        outs = [arr((4, half, width)), arr((heads, length, HD), F32), arr((heads, length, HD), F32)]
    else:
        outs = [arr((4, 2 * half, 3 * width))]
    return order(
        "attn_bwd",
        functools.partial(attn_bwd_kernel, u),
        outs,
        (t, q, k, v, x, *do, *o, *first),
        limit=16,
        scratch=[pltpu.VMEM((heads, 4, half, 2 * HD), BF)] * 2 + [pltpu.VMEM((heads, HD, 4 * half), F32)],
        scalars=1,
    )


def out_kernel(m0, m1, m2, m3, w0, w1, w2, w3, x_ref, bias_ref, gain_ref, shift_ref, resid_ref, n_ref, na_ref, nb_ref):
    half = na_ref.shape[0]
    for u, half_ref in enumerate((na_ref, nb_ref)):
        at = slice(u * half, (u + 1) * half)
        total = sum(dot(m[at], w[...]) for m, w in ((m0, w0), (m1, w1), (m2, w2), (m3, w3)))
        resid = x_ref[at, :].astype(F32) + (total + bias_ref[...])
        resid_ref[at] = resid
        hat, _ = standardized(resid)
        n = (hat * gain_ref[...] + shift_ref[...]).astype(BF)
        n_ref[at] = n
        half_ref[...] = n


def up_kernel(n0, n1, up_ref, act_ref, slope_ref):
    c = 0.7978845608028654
    rows = n0.shape[0]
    step = min(rows, 256)
    for i, n_ref in enumerate((n0, n1)):
        for first in range(0, rows, step):
            at = slice(i * rows + first, i * rows + first + step)
            v = dot(n_ref[first : first + step], up_ref[...])
            square = v * v
            th = jnp.tanh(v * (c + (c * 0.044715) * square))
            half_v = 0.5 * v
            act_ref[at] = (half_v + half_v * th).astype(BF)
            slope_ref[at] = (0.5 + 0.5 * th + half_v * (1.0 - th * th) * (c + (3 * c * 0.044715) * square)).astype(BF)


def back_kernel(u, g0, g1, slope_ref, up_ref, down_ref, dpre_ref, p0, *sends):
    rows = p0.shape[0]
    step = min(rows, 256)
    part = sends[0].shape[0]
    for i, g_ref in enumerate((g0, g1)):
        for first in range(0, rows, step):
            at = slice(i * rows + first, i * rows + first + step)
            g = g_ref[u * rows + first : u * rows + first + step]
            dpre = (dot(g, down_ref[...], NT) * slope_ref[at].astype(F32)).astype(BF)
            dpre_ref[at] = dpre
            total = dot(dpre, up_ref[...], NT).astype(BF)
            if i == 0:
                p0[first : first + step] = total
            elif part < step:
                for n, out_ref in enumerate(sends):
                    out_ref[...] = total[n * part : (n + 1) * part]
            else:
                sends[0][first : first + step] = total


def down_kernel(sources, *refs):
    count = max(i for i, _ in sources) + 1
    acts, w_ref, outs = refs[:count], refs[count], refs[count + 1 :]
    half = outs[0].shape[0] // 2
    rows = outs[1].shape[0]
    for n, (i, first) in enumerate(sources):
        out = dot(acts[i][first : first + half], w_ref[...]).astype(BF)
        if n < 2:
            outs[0][n * half : (n + 1) * half] = out
        elif rows > half:
            outs[1][(n - 2) * half : (n - 1) * half] = out
        else:
            for m in range(half // rows):
                outs[1 + (n - 2) * (half // rows) + m][...] = out[m * rows : (m + 1) * rows]


def mid_kernel(
    u, p0, c1, y2, resid_ref, cot_ref, seg_ref, gain_ref, w0, w1, w2, w3, dresid_ref, dattn_ref, m0, m1, m23, sums_ref
):
    half = y2.shape[0]
    sl = slice(u * half, (u + 1) * half)
    grad = p0[sl].astype(F32) + c1[sl].astype(F32) + y2[...].astype(F32)
    hat, inverse = standardized(resid_ref[sl])
    g = jnp.where(seg_ref[sl] != 0, cot_ref[sl].astype(F32), 0.0)
    dresid = g + norm_back(grad, gain_ref[...], hat, inverse)
    dresid_ref[...] = dresid
    dattn = dresid.astype(BF)
    dattn_ref[...] = dattn
    m0[...] = dot(dattn, w0[...], NT).astype(BF)
    m1[...] = dot(dattn, w1[...], NT).astype(BF)
    m23[:half] = dot(dattn, w2[...], NT).astype(BF)
    m23[half:] = dot(dattn, w3[...], NT).astype(BF)
    rows = [grad * hat, grad, dresid, g]
    sums_ref[...] = jnp.concatenate([jnp.sum(v, 0, keepdims=True) for v in rows] + [jnp.zeros((4, hat.shape[1]), F32)])


def pass_kernel(far_ref, own_ref, out_ref):
    half = own_ref.shape[0]
    out_ref[:half] = far_ref[half:]
    out_ref[half : 2 * half] = own_ref[...]
    if out_ref.shape[0] > 2 * half:
        out_ref[2 * half :] = jnp.zeros((out_ref.shape[0] - 2 * half, own_ref.shape[1]), BF)


def dn1_kernel(pair, g_ref, w_ref, a_ref, *sends):
    width = w_ref.shape[2]
    product = lambda r, at: sum(dot(g_ref[r, at, c * width : (c + 1) * width], w_ref[c], NT) for c in range(3)).astype(BF)
    rows = sends[0].shape[0]
    for i, out_ref in enumerate(sends):
        out_ref[...] = product(2 * pair + 1, slice(i * rows, (i + 1) * rows))
    a_ref[...] = product(2 * pair, slice(0, a_ref.shape[0]))


def last_kernel(p0, c1, y2, x_ref, da, db, gain_ref, out_ref):
    grad = p0[...].astype(F32) + c1[...].astype(F32) + y2[...].astype(F32)
    hat, inverse = standardized(x_ref[...].astype(F32))
    dresid = jnp.where(pl.program_id(0) < 2, da[...], db[...])
    out_ref[...] = dresid + norm_back(grad, gain_ref[...], hat, inverse)


def result_kernel(resid_ref, p0, y2, seg_ref, bias_ref, out_ref):
    total = p0[...].astype(F32) + y2[...].astype(F32)
    out_ref[...] = jnp.where(seg_ref[...] != 0, resid_ref[...] + total + bias_ref[...], 0.0).astype(BF)


def quarters(kinds, size, width):
    rows = size // 4
    maps = {
        "w": lambda i: (i, 0),
        "a": lambda i: (jnp.minimum(i, 1), 0),
        "b": lambda i: (jnp.maximum(i - 2, 0), 0),
        "r": lambda i: (0, 0),
        "s": lambda i: (i, 0),
    }
    specs = [pl.BlockSpec((1 if k == "r" else rows, 1 if k == "s" else width), maps[k]) for k in kinds]
    return specs[:-1], (specs[-1],), (4,)


def order_of(bits):
    rest = [0]
    for bit in reversed(bits[1:]):
        rest = [e | (1 << bit) for e in rest] + rest
    return [e | (1 << bits[0]) for e in rest], rest


def ffn_grad_kernel(bits, tile, count, pairs, d_ref, *refs):
    lefts, rights, outs = refs[:count], refs[count:], refs[-2:]
    single = refs[-1].dtype == F32
    for out_ref, blocks in zip(outs, ([], list(range(8))) if single else order_of(bits)):
        for i, e in enumerate(blocks):
            cols = pl.ds(bits_of(d_ref[0], e, tile), tile)
            total = refs[-3][e] if refs[-3].dtype == F32 else 0.0
            for left, first, rows, right, at in pairs:
                total += dot(lefts[left][first : first + rows, cols], rights[right][at : at + rows], TN)
            out_ref[i] = total.astype(out_ref.dtype)


def ffn_grad(order, name, bits, d, lefts, rights, pairs, so_far=(), more=False):
    tile = lefts[0].shape[1] // 8
    body = functools.partial(ffn_grad_kernel, bits, tile, len(lefts), pairs)
    shape = (tile, rights[0].shape[1])
    outs = [arr((8, *shape), F32)] if more else [arr((4, *shape))] * 2
    return order(name, body, outs, (d, *lefts, *rights, *so_far), scalars=1)


def out_grad_kernel(tile, d_ref, la, lb, m0, m1, m2, m3, send_ref, keep_ref):
    half, width = la.shape[0], m0.shape[1]
    for e in range(8):
        cols = pl.ds(bits_of(d_ref[0], e, tile), tile)
        for r, m in enumerate((m0, m1, m2, m3)):
            total = (dot(la[:, cols], m[:half], TN) + dot(lb[:, cols], m[half:], TN)).astype(BF)
            out_ref = send_ref if r % 2 else keep_ref
            out_ref[e, :, (r // 2) * width : (r // 2 + 1) * width] = total


def qkv_grad_kernel(orders, tile, d_ref, n0, n1, n2, n3, g_ref, w_ref, sums_a, sums_b, gain_ref, shift_ref, keep_ref, got_ref, *refs):
    outs, kept, lines = refs[:4], refs[4], refs[5]
    width = w_ref.shape[2]
    size = g_ref.shape[1]
    count = jnp.ones((8, size), BF)
    weighted, shifted = 0.0, 0.0
    for c in range(3):
        sl = slice(c * width, (c + 1) * width)
        total = sum(dot(n[:size, :], g_ref[r, :, sl], TN) for r, n in enumerate((n0, n1, n2, n3)))
        for s in range(8):
            kept[s ^ d_ref[0], :, sl] = total[s * tile : (s + 1) * tile].astype(BF)
        w = w_ref[c].astype(F32)
        weighted += total * w
        shifted += sum(dot(count, g_ref[r, :, sl]) for r in range(4))[:1] * w
    ones = jnp.ones((8, width), F32)
    high = lambda v: lax.dot_general(ones, v, NT, precision=lax.Precision.HIGHEST, preferred_element_type=F32)
    shift_sum = high(shifted)[:1]
    gain_sum = (high(weighted)[:1] - shift_ref[...] * shift_sum) / gain_ref[...]
    both = sums_a[...] + sums_b[...]
    rows = jnp.concatenate([gain_sum, shift_sum, both[:4], jnp.zeros((10, both.shape[1]), F32)]).astype(BF)
    for s in range(8):
        lines[s ^ d_ref[0]] = rows[:, s * tile : (s + 1) * tile]
    for e in range(8):
        kept[e, :, 3 * width :] = (keep_ref[e].astype(F32) + got_ref[e].astype(F32)).astype(BF)
    first = 0
    for m, bits in enumerate(orders):
        part = outs[2 * m].shape[2]
        for k, blocks in enumerate(order_of(bits)):
            for i, e in enumerate(blocks):
                outs[2 * m + k][i, :tile] = kept[e, :, first : first + part]
                outs[2 * m + k][i, tile:] = jnp.zeros((16, part), BF)
                if m == 0:
                    outs[k][i, tile:, :tile] = lines[e]
        first += part


def add_kernel(*refs):
    first, others, out_ref = refs[0], refs[1:-1], refs[-1]
    at = 0
    for ref in others:
        rows = ref.shape[0]
        out_ref[at : at + rows] = (first[at : at + rows].astype(F32) + ref[...].astype(F32)).astype(BF)
        at += rows


def add_pair_kernel(t_ref, *refs):
    first, others, out_ref = refs[0], refs[1:-1], refs[-1]
    rows = others[0].shape[0] // 2
    theirs = pl.ds(pl.multiple_of(((t_ref[0] & 1) ^ 1) * rows, rows), rows)
    for i, ref in enumerate(others):
        at = slice(i * rows, (i + 1) * rows)
        out_ref[at] = (first[at].astype(F32) + ref[theirs].astype(F32)).astype(BF)


def stage_kernel(turned, groups, later, *refs):
    count = len(turned)
    own, got, outs = refs[:count], refs[count : count + len(groups)], refs[count + len(groups) :]
    total = [None] * count
    for ref, group in zip(got, groups):
        at = 0
        for m in group:
            width = own[m].shape[2]
            total[m] = own[m][...].astype(F32) + ref[:, :, at : at + width].astype(F32)
            at += width
    if not later:
        for m in range(count):
            outs[m][...] = total[m][0].T if turned[m] else total[m][0]
        return
    for ref, group in zip(outs[count:], later):
        at = 0
        for m in group:
            blocks, _, width = total[m].shape
            outs[m][...] = total[m][blocks // 2 :].astype(BF)
            ref[:, :, at : at + width] = total[m][: blocks // 2].astype(BF)
            at += width


def finish_kernel(a_ref, b_ref, got_ref, qkv_ref, own_ref, send_ref, line_ref):
    tile, width = own_ref.shape
    for c in range(5):
        ref, first = (a_ref, c * width) if c < 3 else (b_ref, (c - 3) * width)
        got = got_ref[0, :tile, c * width : (c + 1) * width].astype(F32)
        total = ref[0, :tile, first : first + width].astype(F32) + got
        if c < 3:
            qkv_ref[c] = total
        else:
            (own_ref, send_ref)[c - 3][...] = total
    line_ref[...] = (a_ref[0, tile:, :tile].astype(F32) + got_ref[0, tile:, :tile].astype(F32)).T[:, :8]


def after(x, *others):
    return lax.optimization_barrier((x, *others))[0]


def to_core(x):
    return lax.ppermute(x, "tensor", [(i, i ^ 1) for i in range(4)])


def to_chip(x):
    return lax.ppermute(x, "tensor", [(i, i ^ 2) for i in range(4)])


def to_diag(x):
    return lax.ppermute(x, "tensor", [(i, i ^ 3) for i in range(4)])


def gather(x):
    far = to_chip(x)
    return [x, to_core(x), far, to_core(far)]


def pair_gather(x):
    return lax.all_gather(x, "tensor", axis=0, tiled=True, axis_index_groups=[[0, 1], [2, 3]])


class Reduce:
    def __init__(self, order, dp, d, *matrices):
        self.order, self.dp, self.d = order, dp, d
        self.low = dp.bit_length() - 4
        self.own = [parts[1] for parts, _, _ in matrices]
        self.bits = [list(bits[1:]) for _, bits, _ in matrices]
        self.turned = [turned for _, _, turned in matrices]
        self.groups = [[m] for m in range(len(matrices))]
        self.got = [self.swap(parts[0], bits[0]) for parts, bits, _ in matrices]

    def merge(self, other):
        count = len(self.own)
        self.own, self.bits, self.turned = self.own + other.own, self.bits + other.bits, self.turned + other.turned
        self.groups, self.got = self.groups + [[m + count for m in g] for g in other.groups], self.got + other.got

    def take(self, m):
        other = Reduce(self.order, self.dp, self.d)
        g = self.groups.index([m])
        other.own, other.bits, other.turned = [self.own.pop(m)], [self.bits.pop(m)], [self.turned.pop(m)]
        other.groups, other.got = [[0]], [self.got.pop(g)]
        self.groups.pop(g)
        return other

    def swap(self, x, bit):
        return lax.ppermute(x, "dp", [(i, i ^ (1 << (bit + self.low))) for i in range(self.dp)])

    def stage(self):
        count = len(self.own)
        turned = [bool(f) and not self.low for f in self.turned]
        later = []
        if any(self.bits):
            for key in sorted({(self.bits[m][0], self.own[m].shape[:2]) for m in range(count)}):
                later.append([m for m in range(count) if (self.bits[m][0], self.own[m].shape[:2]) == key])
            outs = [arr((own.shape[0] // 2, *own.shape[1:])) for own in self.own]
            for group in later:
                blocks, rows, _ = outs[group[0]].shape
                outs.append(arr((blocks, rows, sum(self.own[m].shape[2] for m in group))))
        else:
            shapes = [own.shape for own in self.own]
            outs = [arr((s[2], s[1]) if f else s[1:], F32) for s, f in zip(shapes, turned)]
        body = functools.partial(stage_kernel, turned, self.groups, later)
        sums = self.order("stage", body, outs, (*self.own, *self.got))
        if not later:
            return [s if f is None else self.rest(s, f) for s, f in zip(sums, self.turned)]
        self.own = list(sums[:count])
        self.got = [self.swap(x, self.bits[group[0]][0]) for x, group in zip(sums[count:], later)]
        self.groups, self.bits = later, [bits[1:] for bits in self.bits]
        return None

    def rest(self, total, turned):
        for bit in range(self.low - 1, -1, -1):
            mine = (self.d >> bit) & 1
            view = total.reshape(2, total.shape[0] // 2, total.shape[1])
            send = lax.dynamic_index_in_dim(view, 1 - mine, 0, keepdims=False)
            keep = lax.dynamic_index_in_dim(view, mine, 0, keepdims=False)
            total = keep + lax.ppermute(send, "dp", [(i, i ^ (1 << bit)) for i in range(self.dp)])
        return total.T if turned and self.low else total


def place_kernel(rows, d_ref, in_ref, out_ref):
    for i in range(8):
        e = (i & 1) << 2 | (i & 2) | i >> 2
        out_ref[pl.ds(bits_of(d_ref[0], e, rows), rows)] = in_ref[i * rows : (i + 1) * rows]


def local(dp, block_input, segment_ids, w_qkv, w_out, w_up, w_down, ln1_gain, ln1_bias, ln2_gain, ln2_bias, out_bias, down_bias, cotangent):
    size, width = block_input.shape[1:]
    half = size // 2
    hidden = w_up.shape[1]
    local_width = w_qkv.shape[2]
    heads = local_width // HD
    t = lax.axis_index("tensor")
    d = lax.axis_index("dp")
    low = dp.bit_length() - 4
    t_arg = t[None].astype(jnp.int32)
    block_arg = (d >> low)[None].astype(jnp.int32)
    x = block_input[0]
    cot = cotangent[0]
    seg = segment_ids[0][:, None]
    gain1, shift1, gain2, shift2 = ln1_gain[None], ln1_bias[None], ln2_gain[None], ln2_bias[None]
    token = (size, width)
    chunk = (half, width)
    order = Order()

    part = local_width // 8
    wo_part = to_chip(lax.dynamic_slice_in_dim(w_out, (d >> low) * part, part, 0))
    (n1_own,) = order("norm", norm_kernel, [arr((size + 16, width))], (x, segment_ids, gain1, shift1))
    n1_far, n1_core = to_chip(after(n1_own, wo_part)), to_core(n1_own)

    def spread(x, bit):
        sent = lax.ppermute(x, "dp", [(i, i ^ (1 << (bit + low))) for i in range(dp)])
        return jnp.concatenate([x, sent])

    wo_part = spread(order.then(wo_part), 2)
    half_row = [arr((heads, 2 * size, 2 * HD))] * 3
    near = order("qkv", functools.partial(qkv_kernel, 0, heads), half_row, (t_arg, n1_own, n1_core, w_qkv), scalars=1)
    (dffn_own,) = order("masks", masks_kernel, [arr(token)], (cot, seg))
    dffn_core = to_core(dffn_own)
    wo_part = spread(spread(order.then(wo_part), 1), 0)
    body = functools.partial(place_kernel, part)
    (wo_far,) = order("place", body, [arr(w_out.shape)], (block_arg, wo_part), scalars=1)
    wo = [w_out, to_core(order.then(w_out)), wo_far, to_core(wo_far)]
    n1 = [n1_own, n1_core, n1_far, to_core(order.then(n1_far))]
    dffn_far = to_chip(after(dffn_own, n1_far))
    order.wait(wo[1], wo[3])
    args = (t_arg, n1[2], n1[3], w_qkv, *near)
    row = [arr((heads, 4 * size, 2 * HD))] * 3
    q, k, v = order("qkv", functools.partial(qkv_kernel, 2, heads), row, args, scalars=1)

    *o, x_a, x_b = attn_fwd(order, t_arg, q, k, v)
    mixed = [o[0], to_core(o[1]), to_chip(o[2]), to_diag(o[3])]
    args = (*mixed, *wo, x, out_bias[None], gain2, shift2)
    resid, n2_own, n2_a, n2_b = order("out_proj", out_kernel, [arr(token, F32), arr(token)] + [arr(chunk)] * 2, args)
    n2_a = to_chip(n2_a)
    n2_core = to_core(n2_own)
    n2_b = to_chip(n2_b)
    dffn = [dffn_own, dffn_core, dffn_far, to_core(order.then(dffn_far))]
    order.wait(dffn[3])

    def up(first, second):
        outs = [arr((2 * first.shape[0], hidden))] * 2
        return order("up", up_kernel, outs, (first, second, w_up))

    def back(u, grads, slope):
        rows = slope.shape[0] // 2
        sends = [arr((rows, width))] if rows == size else [arr((rows // 2, width))] * 2
        outs = [arr(slope.shape), arr((rows, width)), *sends]
        return order("back", functools.partial(back_kernel, u), outs, (*grads, slope, w_up, w_down))

    act_near, slope = up(n2_own, n2_core)
    dpre_near, p0, p1 = back(0, dffn[:2], slope)
    p1 = to_core(p1)
    n2_a = [n2_a, to_core(order.then(n2_a))]
    order.wait(p1)
    act_a, slope = up(*n2_a)
    dpre_a, p2, *send = back(0, dffn[2:], slope)
    send = [to_core(x) for x in send]
    (chip,) = order("add", add_kernel, [arr(chunk)], (p2, *send))
    chip_a = to_chip(chip)
    bits = ((0, 1, 2), (1, 0, 2))
    pairs = [(0, 0, size, 0, 0), (1, 0, size, 0, size), (2, 0, half, 1, 0), (3, 0, half, 1, half)]
    lefts = [n2_own, n2_core, *n2_a]
    so_far = ffn_grad(order, "up_grad", bits[0], block_arg, lefts, [dpre_near, dpre_a], pairs, more=True)
    n2_b = [n2_b, to_core(order.then(n2_b))]
    act_b, slope = up(*n2_b)
    dpre_b, p2, *send = back(1, dffn[2:], slope)
    send = [pair_gather(x) for x in send]
    (chip,) = order("add", add_pair_kernel, [arr(chunk)], (t_arg, p2, *send), scalars=1)
    chip_b = to_chip(chip)


    def middle(u, y2):
        piece = (half, local_width)
        outs = [arr(chunk, F32), arr(chunk), arr(piece), arr(piece), arr((size, local_width)), arr((8, width), F32)]
        args = (p0, p1, y2, resid, cot, seg, gain2, *wo)
        return order("mid", functools.partial(mid_kernel, u), outs, args)

    def arrived(far, m0, m1, rows, hand_over):
        (send,) = order("pass", pass_kernel, [arr((rows, local_width))], (far, m1))
        got = hand_over(send)
        return m0, got, far, got

    dresid_a, dattn_a, m0a, m1a, send_a, sums_a = middle(0, chip_a)
    far_a = to_chip(send_a)
    pairs = [(i, 0, half, 0, i * half) for i in range(2)]
    parts = ffn_grad(order, "up_grad", bits[0], block_arg, n2_b, [dpre_b], pairs, so_far)
    up_reduce = Reduce(order, dp, d, (parts, bits[0], False))
    pairs = [(0, 0, size, 0, 0), (1, 0, size, 0, size)]
    pairs += [(2 + i, u * half, half, 1 + u, i * half) for u in range(2) for i in range(2)]
    parts = ffn_grad(order, "down_grad", bits[1], block_arg, dffn, [act_near, act_a, act_b], pairs)
    down_reduce = Reduce(order, dp, d, (parts, bits[1], True))
    dresid_b, dattn_b, m0b, m1b, send_b, sums_b = middle(1, chip_b)
    far_b = to_chip(send_b)

    tile = width // 8
    outs = [arr((8, tile, 2 * local_width))] * 2
    args = (block_arg, dattn_a, dattn_b, *mixed)
    out_send, out_keep = order("out_grad", functools.partial(out_grad_kernel, tile), outs, args, scalars=1)
    out_send = to_core(out_send)
    do = arrived(far_a, m0a, m1a, size, pair_gather)
    order.wait(far_b)
    first = attn_bwd(order, 0, t_arg, q, k, v, x_a, do, o)
    do = arrived(far_b, m0b, m1b, 2 * size, to_core)
    up_reduce.stage()
    down_reduce.stage()
    (dqkv,) = attn_bwd(order, 1, t_arg, q, k, v, x_b, do, o, first)
    own, *send = order("dn1", functools.partial(dn1_kernel, 1), [arr(token)] + [arr(chunk)] * 2, (dqkv, w_qkv))
    send = [to_core(x) for x in send]
    up_reduce.merge(down_reduce)
    up_reduce.stage()
    (chip,) = order("add", add_kernel, [arr(token)], (own, *send))
    dn1_chip = to_chip(chip)
    dn1_own, dn1_core = order("dn1", functools.partial(dn1_kernel, 0), [arr(token)] * 2, (dqkv, w_qkv))
    dn1_core = to_core(dn1_core)
    outs = [arr((4, tile + 16, n * local_width)) for n in (3, 3, 2, 2)]
    args = (block_arg, *n1, dqkv, w_qkv, sums_a, sums_b, gain1, shift1, out_keep, out_send)
    scratch = [pltpu.VMEM((8, tile, 5 * local_width), BF), pltpu.VMEM((8, 16, tile), BF)]
    body = functools.partial(qkv_grad_kernel, bits, tile)
    parts = order("qkv_grad", body, outs, args, scratch=scratch, scalars=1)
    qkv_reduce = Reduce(order, dp, d, (parts[:2], bits[0], None), (parts[2:], bits[1], None))
    body = functools.partial(down_kernel, [(0, 0), (1, 0), (0, half), (1, half)])
    fourth = [arr((size // 4, width))] * 4
    ffn2, *send = order("down", body, [arr(token), *fourth], (act_a, act_b, w_down))
    up_sum, down_sum = up_reduce.stage()
    send = [pair_gather(order.then(x)) for x in send]
    order.wait(*send, dn1_core)
    (ffn_chip,) = order("add", add_pair_kernel, [arr(token)], (t_arg, ffn2, *send), scalars=1)
    ffn_chip = to_chip(ffn_chip)
    qkv_reduce.stage()
    blocks = quarters("wwwwabrw", *token)
    args = (dn1_own, dn1_core, dn1_chip, x, dresid_a, dresid_b, gain1)
    (x_grad,) = order("last", last_kernel, [arr(token, F32)], args, blocks=blocks)
    qkv_reduce.stage()
    body = functools.partial(down_kernel, [(0, i * half) for i in range(4)])
    ffn0, *send = order("down", body, [arr(token), *fourth], (act_near, w_down))
    send = [pair_gather(x) for x in send]
    order.wait(*send)
    (ffn0,) = order("add", add_pair_kernel, [arr(token)], (t_arg, ffn0, *send), scalars=1)
    args = (resid, ffn0, ffn_chip, seg, down_bias[None])
    (output,) = order("result", result_kernel, [arr(token)], args, blocks=quarters("wwwsrw", *token))
    chunk = width // dp // 4
    if low:
        first, second = qkv_reduce.stage()
        lines = qkv_reduce.rest(first[tile : tile + 6, :tile].T, False)
        both = jnp.concatenate([qkv_reduce.rest(p[:tile], False) for p in (first, second)], 1)
        qkv_sum = both[:, : 3 * local_width].reshape(width // dp, 3, local_width).transpose(1, 0, 2)
        out_own, out_send = both[:, 3 * local_width : 4 * local_width], both[:, 4 * local_width :]
    else:
        square = (tile, local_width)
        outs = [arr((3, *square), F32), arr(square, F32), arr(square, F32), arr((tile, 8), F32)]
        args = (*qkv_reduce.own, *qkv_reduce.got)
        qkv_sum, out_own, out_send, lines = order("finish", finish_kernel, outs, args)
    out_sum = out_own + to_chip(out_send)
    lines = jnp.sum(lax.all_gather(lines, "tensor", axis=0), 0)
    vectors = lax.dynamic_slice_in_dim(lines, t * chunk, chunk, 0)
    return (output[None], x_grad[None], qkv_sum, out_sum.T, up_sum, down_sum, *(vectors[:, i] for i in range(6)))


def solution(mesh):
    row = P("dp", "tensor", None)
    matrix = (P(None, None, "tensor"), P("tensor", None), P(None, "tensor"), P("tensor", None))
    in_specs = (row, P("dp", "tensor"), *matrix) + (P(),) * 6 + (row,)
    vector = P(("dp", "tensor"))
    out_specs = (row, row, P(None, "dp", "tensor"), P("tensor", "dp"), P("dp", "tensor"), P("tensor", "dp")) + (vector,) * 6
    run = functools.partial(local, mesh.shape["dp"])
    return jax.shard_map(run, mesh=mesh, in_specs=in_specs, out_specs=out_specs, check_vma=False)
```

```python
import functools

import jax
import jax.numpy as jnp
from jax import lax
from jax.experimental import pallas as pl
from jax.experimental.pallas import tpu as pltpu
from jax.sharding import PartitionSpec as P

H = 8
HD = 128
EPS = 1e-05
NEG = -1e30
LOG2E = 1.4426950408889634
BF = jnp.bfloat16
F32 = jnp.float32
NN = (((1,), (0,)), ((), ()))
NT = (((1,), (1,)), ((), ()))
TN = (((0,), (0,)), ((), ()))
VMEM = pl.BlockSpec(memory_space=pltpu.VMEM)
SMEM = pl.BlockSpec(memory_space=pltpu.SMEM)


def dot(a, b, dims=NN):
    return lax.dot_general(a, b, dims, preferred_element_type=F32)


def call(name, body, outs, args, limit=12, scratch=(), scalars=0, blocks=None):
    in_specs, out_specs, grid = blocks or ([SMEM] * scalars + [VMEM] * (len(args) - scalars), (VMEM,) * len(outs), ())
    return pl.pallas_call(
        body,
        out_shape=tuple(outs),
        grid=grid,
        in_specs=in_specs,
        out_specs=out_specs,
        scratch_shapes=list(scratch),
        name=name,
        cost_estimate=pl.CostEstimate(flops=1, bytes_accessed=1, transcendentals=0),
        compiler_params=pltpu.CompilerParams(vmem_limit_bytes=limit * 2**20),
    )(*args)


def arr(shape, dtype=BF):
    return jax.ShapeDtypeStruct(shape, dtype)


def split3(v):
    hi = v.astype(BF)
    rest = v - hi.astype(F32)
    mid = rest.astype(BF)
    return hi, mid, (rest - mid.astype(F32)).astype(BF)


def standardized(values):
    center = values - jnp.mean(values, -1, keepdims=True)
    inverse = lax.rsqrt(jnp.mean(center * center, -1, keepdims=True) + EPS)
    return center * inverse, inverse


def norm_back(grad, gain, hat, inverse):
    e = grad * gain
    return (e - jnp.mean(e, -1, keepdims=True) - hat * jnp.mean(e * hat, -1, keepdims=True)) * inverse


def bits_of(index, place, value):
    return pl.multiple_of((index ^ place) * value, value)


class Order:
    def __init__(self):
        self.last = ()

    def __call__(self, name, body, outs, args, limit=12, scratch=(), scalars=0, blocks=None):
        args = list(args)
        if self.last:
            args[scalars] = after(args[scalars], *self.last)
        got = call(name, body, outs, args, limit, scratch, scalars, blocks)
        self.last = (got[-1],)
        return got

    def then(self, x):
        return after(x, *self.last)

    def wait(self, *values):
        self.last += values


def norm_kernel(x_ref, seg_ref, gain_ref, shift_ref, out_ref):
    size, width = x_ref.shape
    hat, _ = standardized(x_ref[...].astype(F32))
    out_ref[:size] = (hat * gain_ref[...] + shift_ref[...]).astype(BF)
    ids = jnp.broadcast_to(seg_ref[...].astype(F32), (16, size)).astype(BF)
    out_ref[size:, :size] = ids
    out_ref[size:, size:] = jnp.zeros((16, width - size), BF)


def masks_kernel(cot_ref, seg_ref, out_ref):
    out_ref[...] = jnp.where(seg_ref[...] != 0, cot_ref[...], jnp.zeros((), BF))


def qkv_kernel(r0, heads, t_ref, n0, n1, w_ref, *refs):
    size = n0.shape[0] - 16
    t = t_ref[0]
    q_ref, k_ref, v_ref = refs[-3:]
    base_row = 0
    if len(refs) > 3:
        mine = pl.ds(pl.multiple_of((t >> 1) * (2 * size), size), 2 * size)
        for given, out_ref in zip(refs[:3], refs[3:]):
            out_ref[:, mine, :] = given[...]
        base_row = ((t >> 1) ^ 1) * (2 * size)
    lane = lax.broadcasted_iota(jnp.int32, (size, HD), 1)
    row = lax.broadcasted_iota(jnp.int32, (size, HD), 0)
    article = (lane >= 3) & (lane < 7)
    v_more = jnp.where(lane < 3, 1.0, 0.0).astype(BF)
    for r, n_ref in ((r0, n0), (r0 + 1, n1)):
        n = n_ref[:size]
        place = ((t ^ r) * size + row).astype(F32)
        ids = jnp.broadcast_to(n_ref[size:, :size].astype(F32)[:1], (HD, size)).T
        hot = ids == (lane - 3).astype(F32)
        q_more = jnp.where((lane < 3) | (article & hot), 1.0, 0.0).astype(BF)
        base = jnp.where(article, jnp.where(hot, 0.0, NEG), jnp.where((lane >= 7) & (lane < 10), 1.0, 0.0))
        q = (dot(n, w_ref[0]) * (HD**-0.5 * LOG2E)).astype(BF)
        k = dot(n, w_ref[1]).astype(BF)
        v = dot(n, w_ref[2]).astype(BF)
        at = pl.ds(pl.multiple_of(base_row + ((t ^ r) & 1) * size, size), size)
        for h in range(heads):
            power = jnp.full((size, HD), (t * heads + h + 1).astype(F32) * (-8.0 / H), F32)
            hi, mid, lo = split3(jnp.exp2(power) * LOG2E * place)
            more = jnp.where(lane == 0, hi, jnp.where(lane == 1, mid, jnp.where(lane == 2, lo, base.astype(BF))))
            sl = slice(h * HD, (h + 1) * HD)
            q_ref[h, at, :HD] = q[:, sl]
            q_ref[h, at, HD:] = q_more
            k_ref[h, at, :HD] = k[:, sl]
            k_ref[h, at, HD:] = more
            v_ref[h, at, :HD] = v[:, sl]
            v_ref[h, at, HD:] = v_more


def attn_fwd_kernel(t_ref, q_ref, k_ref, v_ref, m0, m1, m2, m3, xa_ref, xb_ref, kept):
    heads, length, _ = q_ref.shape
    half = length // 8
    t = t_ref[0]
    row = lax.broadcasted_iota(jnp.int32, (half, half), 0)
    col = lax.broadcasted_iota(jnp.int32, (half, half), 1)
    keep = col <= row
    lane = lax.broadcasted_iota(jnp.int32, (half, HD), 1)
    for block in range(8):
        p, u = block // 2, block % 2
        start = block * half
        end = start + half
        for h in range(heads):
            q = q_ref[h, start:end, :]
            near = jnp.where(keep, dot(q, k_ref[h, start:end, :], NT), NEG)
            top = jnp.max(near, -1, keepdims=True)
            if start:
                far = dot(q, k_ref[h, :start, :], NT)
                top = jnp.maximum(top, jnp.max(far, -1, keepdims=True))
            out = dot(jnp.exp2(near - top).astype(BF), v_ref[h, start:end, :])
            if start:
                out = out + dot(jnp.exp2(far - top).astype(BF), v_ref[h, :start, :])
            total = out[:, HD : HD + 1]
            kept[p ^ t, u * half : (u + 1) * half, h * HD : (h + 1) * HD] = (out[:, :HD] / total).astype(BF)
            hi, mid, lo = split3(-(top + jnp.log2(total)))
            more = jnp.where(lane == 7, hi, jnp.where(lane == 8, mid, jnp.where(lane == 9, lo, q[:, HD:])))
            (xa_ref, xb_ref)[u][h, p] = more
    for r, out_ref in enumerate((m0, m1, m2, m3)):
        out_ref[...] = kept[r]


def attn_fwd(order, t, q, k, v):
    heads, length, _ = q.shape
    size = length // 4
    outs = [arr((size, heads * HD))] * 4 + [arr((heads, 4, size // 2, HD))] * 2
    scratch = [pltpu.VMEM((4, size, heads * HD), BF)]
    return order("attn_fwd", attn_fwd_kernel, outs, (t, q, k, v), limit=10, scratch=scratch, scalars=1)


def attn_bwd_kernel(u, t_ref, q_ref, k_ref, v_ref, x_ref, *rest):
    do_refs, o_refs, rest = rest[:4], rest[4:8], rest[8:]
    heads, length, _ = q_ref.shape
    half = length // 8
    pick = lambda ref, sl: ref[u * half : (u + 1) * half, sl]
    size = 2 * half
    width = heads * HD
    if u == 0:
        dq_ref, dk_ref, dv_ref, qs, ds, dqt = rest
    else:
        dq_first, dk_first, dv_first, g_ref, qs, ds, dqt = rest
    t = t_ref[0]
    lane = lax.broadcasted_iota(jnp.int32, (half, HD), 1)
    for h in range(heads):
        sl = slice(h * HD, (h + 1) * HD)
        for p in range(4):
            qs[h, p, :, :HD] = q_ref[h, (2 * p + u) * half : (2 * p + u + 1) * half, :HD]
            qs[h, p, :, HD:] = x_ref[h, p]
        for r in range(4):
            if r % 2:
                other = (((t & 1) ^ 1) * size if u == 0 else 0) + (half if r == 1 else 0)
                do = do_refs[r][pl.ds(pl.multiple_of(other, half), half), sl]
            else:
                do = do_refs[r][:half, sl]
            delta = jnp.sum(do.astype(F32) * pick(o_refs[r], sl).astype(F32), -1, keepdims=True)
            hi, mid, lo = split3(-delta)
            ds[h, r ^ t, :, :HD] = do
            ds[h, r ^ t, :, HD:] = jnp.where(
                lane == 0, hi, jnp.where(lane == 1, mid, jnp.where(lane == 2, lo, jnp.zeros_like(hi)))
            )
    near_rows = half * (1 + u)
    row = lax.broadcasted_iota(jnp.int32, (near_rows, half), 0)
    col = lax.broadcasted_iota(jnp.int32, (near_rows, half), 1)
    keep = row <= col + u * half
    for p in range(4):
        for h in range(heads):

            def part(rows, first, last, masked):
                at = slice(p * size, p * size + rows)
                n = (last - first) * half
                q = qs[h, first:last].reshape(n, 2 * HD)
                do = ds[h, first:last].reshape(n, 2 * HD)
                s = dot(k_ref[h, at, :], q, NT)
                if masked:
                    s = jnp.where(keep, s, NEG)
                e = jnp.exp2(s)
                de = (e * dot(v_ref[h, at, :], do, NT)).astype(BF)
                dv = dot(e.astype(BF), do[:, :HD])
                dk = dot(de, q[:, :HD])
                dq = dot(k_ref[h, at, :HD], de, TN)
                cols = slice(first * half, last * half)
                if p:
                    dqt[h, :, cols] += dq
                else:
                    dqt[h, :, cols] = dq
                return dk, dv

            dk, dv = part(near_rows, p, p + 1, True)
            if p < 3:
                dk_far, dv_far = part(size, p + 1, 4, False)
                if near_rows < size:
                    pad = jnp.zeros((size - near_rows, HD), F32)
                    dk, dv = jnp.concatenate([dk, pad]), jnp.concatenate([dv, pad])
                dk, dv = dk + dk_far, dv + dv_far
            elif near_rows < size:
                pad = jnp.zeros((size - near_rows, HD), F32)
                dk, dv = jnp.concatenate([dk, pad]), jnp.concatenate([dv, pad])
            dq = (dqt[h, :, p * half : (p + 1) * half].T * HD**-0.5).astype(BF)
            sl = slice(h * HD, (h + 1) * HD)
            if u == 0:
                dk_ref[h, p * size : (p + 1) * size] = dk
                dv_ref[h, p * size : (p + 1) * size] = dv
                dq_ref[p ^ t, :, sl] = dq
            else:
                at = slice(p * size, (p + 1) * size)
                g_ref[p ^ t, half:, sl] = dq
                g_ref[p ^ t, :, width + h * HD : width + (h + 1) * HD] = (
                    (dk + dk_first[h, at]) * (1.0 / LOG2E)
                ).astype(BF)
                g_ref[p ^ t, :, 2 * width + h * HD : 2 * width + (h + 1) * HD] = (dv + dv_first[h, at]).astype(BF)
    if u == 1:
        for r in range(4):
            g_ref[r, :half, :width] = dq_first[r]


def attn_bwd(order, u, t, q, k, v, x, do, o, first=()):
    heads, length, _ = q.shape
    half = length // 8
    width = heads * HD
    if u == 0:
        outs = [arr((4, half, width)), arr((heads, length, HD), F32), arr((heads, length, HD), F32)]
    else:
        outs = [arr((4, 2 * half, 3 * width))]
    return order(
        "attn_bwd",
        functools.partial(attn_bwd_kernel, u),
        outs,
        (t, q, k, v, x, *do, *o, *first),
        limit=16,
        scratch=[pltpu.VMEM((heads, 4, half, 2 * HD), BF)] * 2 + [pltpu.VMEM((heads, HD, 4 * half), F32)],
        scalars=1,
    )


def out_kernel(m0, m1, m2, m3, w0, w1, w2, w3, x_ref, bias_ref, gain_ref, shift_ref, resid_ref, n_ref, na_ref, nb_ref):
    half = na_ref.shape[0]
    for u, half_ref in enumerate((na_ref, nb_ref)):
        at = slice(u * half, (u + 1) * half)
        total = sum(dot(m[at], w[...]) for m, w in ((m0, w0), (m1, w1), (m2, w2), (m3, w3)))
        resid = x_ref[at, :].astype(F32) + (total + bias_ref[...])
        resid_ref[at] = resid
        hat, _ = standardized(resid)
        n = (hat * gain_ref[...] + shift_ref[...]).astype(BF)
        n_ref[at] = n
        half_ref[...] = n


def up_kernel(n0, n1, up_ref, act_ref, slope_ref):
    c = 0.7978845608028654
    rows = n0.shape[0]
    step = min(rows, 256)
    for i, n_ref in enumerate((n0, n1)):
        for first in range(0, rows, step):
            at = slice(i * rows + first, i * rows + first + step)
            v = dot(n_ref[first : first + step], up_ref[...])
            square = v * v
            th = jnp.tanh(v * (c + (c * 0.044715) * square))
            half_v = 0.5 * v
            act_ref[at] = (half_v + half_v * th).astype(BF)
            slope_ref[at] = (0.5 + 0.5 * th + half_v * (1.0 - th * th) * (c + (3 * c * 0.044715) * square)).astype(BF)


def back_kernel(u, g0, g1, slope_ref, up_ref, down_ref, dpre_ref, p0, *sends):
    rows = p0.shape[0]
    step = min(rows, 256)
    part = sends[0].shape[0]
    for i, g_ref in enumerate((g0, g1)):
        for first in range(0, rows, step):
            at = slice(i * rows + first, i * rows + first + step)
            g = g_ref[u * rows + first : u * rows + first + step]
            dpre = (dot(g, down_ref[...], NT) * slope_ref[at].astype(F32)).astype(BF)
            dpre_ref[at] = dpre
            total = dot(dpre, up_ref[...], NT).astype(BF)
            if i == 0:
                p0[first : first + step] = total
            elif part < step:
                for n, out_ref in enumerate(sends):
                    out_ref[...] = total[n * part : (n + 1) * part]
            else:
                sends[0][first : first + step] = total


def down_kernel(sources, *refs):
    count = max(i for i, _ in sources) + 1
    acts, w_ref, outs = refs[:count], refs[count], refs[count + 1 :]
    half = outs[0].shape[0] // 2
    rows = outs[1].shape[0]
    for n, (i, first) in enumerate(sources):
        out = dot(acts[i][first : first + half], w_ref[...]).astype(BF)
        if n < 2:
            outs[0][n * half : (n + 1) * half] = out
        elif rows > half:
            outs[1][(n - 2) * half : (n - 1) * half] = out
        else:
            for m in range(half // rows):
                outs[1 + (n - 2) * (half // rows) + m][...] = out[m * rows : (m + 1) * rows]


def mid_kernel(
    u, p0, c1, y2, resid_ref, cot_ref, seg_ref, gain_ref, w0, w1, w2, w3, dresid_ref, dattn_ref, m0, m1, m23, sums_ref
):
    half = y2.shape[0]
    sl = slice(u * half, (u + 1) * half)
    grad = p0[sl].astype(F32) + c1[sl].astype(F32) + y2[...].astype(F32)
    hat, inverse = standardized(resid_ref[sl])
    g = jnp.where(seg_ref[sl] != 0, cot_ref[sl].astype(F32), 0.0)
    dresid = g + norm_back(grad, gain_ref[...], hat, inverse)
    dresid_ref[...] = dresid
    dattn = dresid.astype(BF)
    dattn_ref[...] = dattn
    m0[...] = dot(dattn, w0[...], NT).astype(BF)
    m1[...] = dot(dattn, w1[...], NT).astype(BF)
    m23[:half] = dot(dattn, w2[...], NT).astype(BF)
    m23[half:] = dot(dattn, w3[...], NT).astype(BF)
    rows = [grad * hat, grad, dresid, g]
    sums_ref[...] = jnp.concatenate([jnp.sum(v, 0, keepdims=True) for v in rows] + [jnp.zeros((4, hat.shape[1]), F32)])


def pass_kernel(far_ref, own_ref, out_ref):
    half = own_ref.shape[0]
    out_ref[:half] = far_ref[half:]
    out_ref[half : 2 * half] = own_ref[...]
    if out_ref.shape[0] > 2 * half:
        out_ref[2 * half :] = jnp.zeros((out_ref.shape[0] - 2 * half, own_ref.shape[1]), BF)


def dn1_kernel(pair, g_ref, w_ref, a_ref, *sends):
    width = w_ref.shape[2]
    product = lambda r, at: sum(dot(g_ref[r, at, c * width : (c + 1) * width], w_ref[c], NT) for c in range(3)).astype(BF)
    rows = sends[0].shape[0]
    for i, out_ref in enumerate(sends):
        out_ref[...] = product(2 * pair + 1, slice(i * rows, (i + 1) * rows))
    a_ref[...] = product(2 * pair, slice(0, a_ref.shape[0]))


def last_kernel(p0, c1, y2, x_ref, da, db, gain_ref, out_ref):
    grad = p0[...].astype(F32) + c1[...].astype(F32) + y2[...].astype(F32)
    hat, inverse = standardized(x_ref[...].astype(F32))
    dresid = jnp.where(pl.program_id(0) < 2, da[...], db[...])
    out_ref[...] = dresid + norm_back(grad, gain_ref[...], hat, inverse)


def result_kernel(resid_ref, p0, y2, seg_ref, bias_ref, out_ref):
    total = p0[...].astype(F32) + y2[...].astype(F32)
    out_ref[...] = jnp.where(seg_ref[...] != 0, resid_ref[...] + total + bias_ref[...], 0.0).astype(BF)


def quarters(kinds, size, width):
    rows = size // 4
    maps = {
        "w": lambda i: (i, 0),
        "a": lambda i: (jnp.minimum(i, 1), 0),
        "b": lambda i: (jnp.maximum(i - 2, 0), 0),
        "r": lambda i: (0, 0),
        "s": lambda i: (i, 0),
    }
    specs = [pl.BlockSpec((1 if k == "r" else rows, 1 if k == "s" else width), maps[k]) for k in kinds]
    return specs[:-1], (specs[-1],), (4,)


def order_of(bits):
    rest = [0]
    for bit in reversed(bits[1:]):
        rest = [e | (1 << bit) for e in rest] + rest
    return [e | (1 << bits[0]) for e in rest], rest


def ffn_grad_kernel(bits, tile, count, pairs, d_ref, *refs):
    lefts, rights, outs = refs[:count], refs[count:], refs[-2:]
    single = refs[-1].dtype == F32
    for out_ref, blocks in zip(outs, ([], list(range(8))) if single else order_of(bits)):
        for i, e in enumerate(blocks):
            cols = pl.ds(bits_of(d_ref[0], e, tile), tile)
            total = refs[-3][e] if refs[-3].dtype == F32 else 0.0
            for left, first, rows, right, at in pairs:
                total += dot(lefts[left][first : first + rows, cols], rights[right][at : at + rows], TN)
            out_ref[i] = total.astype(out_ref.dtype)


def ffn_grad(order, name, bits, d, lefts, rights, pairs, so_far=(), more=False):
    tile = lefts[0].shape[1] // 8
    body = functools.partial(ffn_grad_kernel, bits, tile, len(lefts), pairs)
    shape = (tile, rights[0].shape[1])
    outs = [arr((8, *shape), F32)] if more else [arr((4, *shape))] * 2
    return order(name, body, outs, (d, *lefts, *rights, *so_far), scalars=1)


def out_grad_kernel(tile, d_ref, la, lb, m0, m1, m2, m3, send_ref, keep_ref):
    half, width = la.shape[0], m0.shape[1]
    for e in range(8):
        cols = pl.ds(bits_of(d_ref[0], e, tile), tile)
        for r, m in enumerate((m0, m1, m2, m3)):
            total = (dot(la[:, cols], m[:half], TN) + dot(lb[:, cols], m[half:], TN)).astype(BF)
            out_ref = send_ref if r % 2 else keep_ref
            out_ref[e, :, (r // 2) * width : (r // 2 + 1) * width] = total


def qkv_grad_kernel(orders, tile, d_ref, n0, n1, n2, n3, g_ref, w_ref, sums_a, sums_b, gain_ref, shift_ref, keep_ref, got_ref, *refs):
    outs, kept, lines = refs[:4], refs[4], refs[5]
    width = w_ref.shape[2]
    size = g_ref.shape[1]
    count = jnp.ones((8, size), BF)
    weighted, shifted = 0.0, 0.0
    for c in range(3):
        sl = slice(c * width, (c + 1) * width)
        total = sum(dot(n[:size, :], g_ref[r, :, sl], TN) for r, n in enumerate((n0, n1, n2, n3)))
        for s in range(8):
            kept[s ^ d_ref[0], :, sl] = total[s * tile : (s + 1) * tile].astype(BF)
        w = w_ref[c].astype(F32)
        weighted += total * w
        shifted += sum(dot(count, g_ref[r, :, sl]) for r in range(4))[:1] * w
    ones = jnp.ones((8, width), F32)
    high = lambda v: lax.dot_general(ones, v, NT, precision=lax.Precision.HIGHEST, preferred_element_type=F32)
    shift_sum = high(shifted)[:1]
    gain_sum = (high(weighted)[:1] - shift_ref[...] * shift_sum) / gain_ref[...]
    both = sums_a[...] + sums_b[...]
    rows = jnp.concatenate([gain_sum, shift_sum, both[:4], jnp.zeros((10, both.shape[1]), F32)]).astype(BF)
    for s in range(8):
        lines[s ^ d_ref[0]] = rows[:, s * tile : (s + 1) * tile]
    for m, bits in enumerate(orders):
        part = outs[2 * m].shape[2]
        for k, blocks in enumerate(order_of(bits)):
            for i, e in enumerate(blocks):
                if m == 0:
                    outs[k][i, :tile] = kept[e]
                else:
                    outs[2 + k][i, :tile] = (keep_ref[e].astype(F32) + got_ref[e].astype(F32)).astype(BF)
                outs[2 * m + k][i, tile:] = jnp.zeros((16, part), BF)
                if m == 0:
                    outs[k][i, tile:, :tile] = lines[e]


def add_kernel(*refs):
    first, others, out_ref = refs[0], refs[1:-1], refs[-1]
    at = 0
    for ref in others:
        rows = ref.shape[0]
        out_ref[at : at + rows] = (first[at : at + rows].astype(F32) + ref[...].astype(F32)).astype(BF)
        at += rows


def add_pair_kernel(t_ref, *refs):
    first, others, out_ref = refs[0], refs[1:-1], refs[-1]
    rows = others[0].shape[0] // 2
    theirs = pl.ds(pl.multiple_of(((t_ref[0] & 1) ^ 1) * rows, rows), rows)
    for i, ref in enumerate(others):
        at = slice(i * rows, (i + 1) * rows)
        out_ref[at] = (first[at].astype(F32) + ref[theirs].astype(F32)).astype(BF)


def stage_kernel(turned, groups, later, *refs):
    count = len(turned)
    own, got, outs = refs[:count], refs[count : count + len(groups)], refs[count + len(groups) :]
    total = [None] * count
    for ref, group in zip(got, groups):
        at = 0
        for m in group:
            width = own[m].shape[2]
            total[m] = own[m][...].astype(F32) + ref[:, :, at : at + width].astype(F32)
            at += width
    if not later:
        for m in range(count):
            outs[m][...] = total[m][0].T if turned[m] else total[m][0]
        return
    for ref, group in zip(outs[count:], later):
        at = 0
        for m in group:
            blocks, _, width = total[m].shape
            outs[m][...] = total[m][blocks // 2 :].astype(BF)
            ref[:, :, at : at + width] = total[m][: blocks // 2].astype(BF)
            at += width


def finish_kernel(a_ref, b_ref, got_ref, qkv_ref, own_ref, send_ref, line_ref):
    tile, width = own_ref.shape
    for c in range(5):
        ref, first = (a_ref, c * width) if c < 3 else (b_ref, (c - 3) * width)
        got = got_ref[0, :tile, c * width : (c + 1) * width].astype(F32)
        total = ref[0, :tile, first : first + width].astype(F32) + got
        if c < 3:
            qkv_ref[c] = total
        else:
            out_ref = (own_ref, send_ref)[c - 3]
            out_ref[...] = total.astype(out_ref.dtype)
    line_ref[...] = (a_ref[0, tile:, :tile].astype(F32) + got_ref[0, tile:, :tile].astype(F32)).T[:, :8]


def after(x, *others):
    return lax.optimization_barrier((x, *others))[0]


def to_core(x):
    return lax.ppermute(x, "tensor", [(i, i ^ 1) for i in range(4)])


def to_chip(x):
    return lax.ppermute(x, "tensor", [(i, i ^ 2) for i in range(4)])


def to_diag(x):
    return lax.ppermute(x, "tensor", [(i, i ^ 3) for i in range(4)])


def gather(x):
    far = to_chip(x)
    return [x, to_core(x), far, to_core(far)]


def pair_gather(x):
    return lax.all_gather(x, "tensor", axis=0, tiled=True, axis_index_groups=[[0, 1], [2, 3]])


class Reduce:
    def __init__(self, order, dp, d, *matrices):
        self.order, self.dp, self.d = order, dp, d
        self.low = dp.bit_length() - 4
        self.own = [parts[1] for parts, _, _ in matrices]
        self.bits = [list(bits[1:]) for _, bits, _ in matrices]
        self.turned = [turned for _, _, turned in matrices]
        self.groups = [[m] for m in range(len(matrices))]
        self.got = [self.swap(parts[0], bits[0]) for parts, bits, _ in matrices]

    def merge(self, other):
        count = len(self.own)
        self.own, self.bits, self.turned = self.own + other.own, self.bits + other.bits, self.turned + other.turned
        self.groups, self.got = self.groups + [[m + count for m in g] for g in other.groups], self.got + other.got

    def take(self, m):
        other = Reduce(self.order, self.dp, self.d)
        g = self.groups.index([m])
        other.own, other.bits, other.turned = [self.own.pop(m)], [self.bits.pop(m)], [self.turned.pop(m)]
        other.groups, other.got = [[0]], [self.got.pop(g)]
        self.groups.pop(g)
        return other

    def swap(self, x, bit):
        return lax.ppermute(x, "dp", [(i, i ^ (1 << (bit + self.low))) for i in range(self.dp)])

    def stage(self):
        count = len(self.own)
        turned = [bool(f) and not self.low for f in self.turned]
        later = []
        if any(self.bits):
            for key in sorted({(self.bits[m][0], self.own[m].shape[:2]) for m in range(count)}):
                later.append([m for m in range(count) if (self.bits[m][0], self.own[m].shape[:2]) == key])
            outs = [arr((own.shape[0] // 2, *own.shape[1:])) for own in self.own]
            for group in later:
                blocks, rows, _ = outs[group[0]].shape
                outs.append(arr((blocks, rows, sum(self.own[m].shape[2] for m in group))))
        else:
            shapes = [own.shape for own in self.own]
            outs = [arr((s[2], s[1]) if f else s[1:], F32) for s, f in zip(shapes, turned)]
        body = functools.partial(stage_kernel, turned, self.groups, later)
        sums = self.order("stage", body, outs, (*self.own, *self.got))
        if not later:
            return [s if f is None else self.rest(s, f) for s, f in zip(sums, self.turned)]
        self.own = list(sums[:count])
        self.got = [self.swap(x, self.bits[group[0]][0]) for x, group in zip(sums[count:], later)]
        self.groups, self.bits = later, [bits[1:] for bits in self.bits]
        return None

    def rest(self, total, turned):
        for bit in range(self.low - 1, -1, -1):
            mine = (self.d >> bit) & 1
            view = total.reshape(2, total.shape[0] // 2, total.shape[1])
            send = lax.dynamic_index_in_dim(view, 1 - mine, 0, keepdims=False)
            keep = lax.dynamic_index_in_dim(view, mine, 0, keepdims=False)
            total = keep + lax.ppermute(send, "dp", [(i, i ^ (1 << bit)) for i in range(self.dp)])
        return total.T if turned and self.low else total


def place_kernel(rows, d_ref, in_ref, out_ref):
    for i in range(8):
        e = (i & 1) << 2 | (i & 2) | i >> 2
        out_ref[pl.ds(bits_of(d_ref[0], e, rows), rows)] = in_ref[i * rows : (i + 1) * rows]


def local(dp, block_input, segment_ids, w_qkv, w_out, w_up, w_down, ln1_gain, ln1_bias, ln2_gain, ln2_bias, out_bias, down_bias, cotangent):
    size, width = block_input.shape[1:]
    half = size // 2
    hidden = w_up.shape[1]
    local_width = w_qkv.shape[2]
    heads = local_width // HD
    t = lax.axis_index("tensor")
    d = lax.axis_index("dp")
    low = dp.bit_length() - 4
    t_arg = t[None].astype(jnp.int32)
    block_arg = (d >> low)[None].astype(jnp.int32)
    x = block_input[0]
    cot = cotangent[0]
    seg = segment_ids[0][:, None]
    gain1, shift1, gain2, shift2 = ln1_gain[None], ln1_bias[None], ln2_gain[None], ln2_bias[None]
    token = (size, width)
    chunk = (half, width)
    order = Order()

    part = local_width // 8
    wo_part = to_chip(lax.dynamic_slice_in_dim(w_out, (d >> low) * part, part, 0))
    (n1_own,) = order("norm", norm_kernel, [arr((size + 16, width))], (x, segment_ids, gain1, shift1))
    n1_far, n1_core = to_chip(after(n1_own, wo_part)), to_core(n1_own)

    def spread(x, bit):
        sent = lax.ppermute(x, "dp", [(i, i ^ (1 << (bit + low))) for i in range(dp)])
        return jnp.concatenate([x, sent])

    wo_part = spread(order.then(wo_part), 2)
    half_row = [arr((heads, 2 * size, 2 * HD))] * 3
    near = order("qkv", functools.partial(qkv_kernel, 0, heads), half_row, (t_arg, n1_own, n1_core, w_qkv), scalars=1)
    (dffn_own,) = order("masks", masks_kernel, [arr(token)], (cot, seg))
    dffn_core = to_core(dffn_own)
    wo_part = spread(spread(order.then(wo_part), 1), 0)
    body = functools.partial(place_kernel, part)
    (wo_far,) = order("place", body, [arr(w_out.shape)], (block_arg, wo_part), scalars=1)
    wo = [w_out, to_core(order.then(w_out)), wo_far, to_core(wo_far)]
    n1 = [n1_own, n1_core, n1_far, to_core(order.then(n1_far))]
    dffn_far = to_chip(after(dffn_own, n1_far))
    order.wait(wo[1], wo[3])
    args = (t_arg, n1[2], n1[3], w_qkv, *near)
    row = [arr((heads, 4 * size, 2 * HD))] * 3
    q, k, v = order("qkv", functools.partial(qkv_kernel, 2, heads), row, args, scalars=1)

    *o, x_a, x_b = attn_fwd(order, t_arg, q, k, v)
    mixed = [o[0], to_core(o[1]), to_chip(o[2]), to_diag(o[3])]
    args = (*mixed, *wo, x, out_bias[None], gain2, shift2)
    resid, n2_own, n2_a, n2_b = order("out_proj", out_kernel, [arr(token, F32), arr(token)] + [arr(chunk)] * 2, args)
    n2_a = to_chip(n2_a)
    n2_core = to_core(n2_own)
    n2_b = to_chip(n2_b)
    dffn = [dffn_own, dffn_core, dffn_far, to_core(order.then(dffn_far))]
    order.wait(dffn[3])

    def up(first, second):
        outs = [arr((2 * first.shape[0], hidden))] * 2
        return order("up", up_kernel, outs, (first, second, w_up))

    def back(u, grads, slope):
        rows = slope.shape[0] // 2
        sends = [arr((rows, width))] if rows == size else [arr((rows // 2, width))] * 2
        outs = [arr(slope.shape), arr((rows, width)), *sends]
        return order("back", functools.partial(back_kernel, u), outs, (*grads, slope, w_up, w_down))

    act_near, slope = up(n2_own, n2_core)
    dpre_near, p0, p1 = back(0, dffn[:2], slope)
    p1 = to_core(p1)
    n2_a = [n2_a, to_core(order.then(n2_a))]
    order.wait(p1)
    act_a, slope = up(*n2_a)
    dpre_a, p2, *send = back(0, dffn[2:], slope)
    send = [to_core(x) for x in send]
    (chip,) = order("add", add_kernel, [arr(chunk)], (p2, *send))
    chip_a = to_chip(chip)
    bits = ((0, 1, 2), (1, 0, 2))
    pairs = [(0, 0, size, 0, 0), (1, 0, size, 0, size), (2, 0, half, 1, 0), (3, 0, half, 1, half)]
    lefts = [n2_own, n2_core, *n2_a]
    so_far = ffn_grad(order, "up_grad", bits[0], block_arg, lefts, [dpre_near, dpre_a], pairs, more=True)
    n2_b = [n2_b, to_core(order.then(n2_b))]
    act_b, slope = up(*n2_b)
    dpre_b, p2, *send = back(1, dffn[2:], slope)
    send = [pair_gather(x) for x in send]
    (chip,) = order("add", add_pair_kernel, [arr(chunk)], (t_arg, p2, *send), scalars=1)
    chip_b = to_chip(chip)


    def middle(u, y2):
        piece = (half, local_width)
        outs = [arr(chunk, F32), arr(chunk), arr(piece), arr(piece), arr((size, local_width)), arr((8, width), F32)]
        args = (p0, p1, y2, resid, cot, seg, gain2, *wo)
        return order("mid", functools.partial(mid_kernel, u), outs, args)

    def arrived(far, m0, m1, rows, hand_over):
        (send,) = order("pass", pass_kernel, [arr((rows, local_width))], (far, m1))
        got = hand_over(send)
        return m0, got, far, got

    dresid_a, dattn_a, m0a, m1a, send_a, sums_a = middle(0, chip_a)
    far_a = to_chip(send_a)
    pairs = [(i, 0, half, 0, i * half) for i in range(2)]
    parts = ffn_grad(order, "up_grad", bits[0], block_arg, n2_b, [dpre_b], pairs, so_far)
    up_reduce = Reduce(order, dp, d, (parts, bits[0], False))
    pairs = [(0, 0, size, 0, 0), (1, 0, size, 0, size)]
    pairs += [(2 + i, u * half, half, 1 + u, i * half) for u in range(2) for i in range(2)]
    parts = ffn_grad(order, "down_grad", bits[1], block_arg, dffn, [act_near, act_a, act_b], pairs)
    down_reduce = Reduce(order, dp, d, (parts, bits[1], True))
    dresid_b, dattn_b, m0b, m1b, send_b, sums_b = middle(1, chip_b)
    far_b = to_chip(send_b)

    tile = width // 8
    outs = [arr((8, tile, 2 * local_width))] * 2
    args = (block_arg, dattn_a, dattn_b, *mixed)
    out_send, out_keep = order("out_grad", functools.partial(out_grad_kernel, tile), outs, args, scalars=1)
    out_send = to_core(out_send)
    do = arrived(far_a, m0a, m1a, size, pair_gather)
    order.wait(far_b)
    first = attn_bwd(order, 0, t_arg, q, k, v, x_a, do, o)
    do = arrived(far_b, m0b, m1b, 2 * size, to_core)
    up_reduce.stage()
    down_reduce.stage()
    (dqkv,) = attn_bwd(order, 1, t_arg, q, k, v, x_b, do, o, first)
    own, *send = order("dn1", functools.partial(dn1_kernel, 1), [arr(token)] + [arr(chunk)] * 2, (dqkv, w_qkv))
    send = [to_core(x) for x in send]
    up_reduce.merge(down_reduce)
    up_reduce.stage()
    (chip,) = order("add", add_kernel, [arr(token)], (own, *send))
    dn1_chip = to_chip(chip)
    dn1_own, dn1_core = order("dn1", functools.partial(dn1_kernel, 0), [arr(token)] * 2, (dqkv, w_qkv))
    dn1_core = to_core(dn1_core)
    outs = [arr((4, tile + 16, n * local_width)) for n in (3, 3, 2, 2)]
    args = (block_arg, *n1, dqkv, w_qkv, sums_a, sums_b, gain1, shift1, out_keep, out_send)
    scratch = [pltpu.VMEM((8, tile, 3 * local_width), BF), pltpu.VMEM((8, 16, tile), BF)]
    body = functools.partial(qkv_grad_kernel, bits, tile)
    parts = order("qkv_grad", body, outs, args, scratch=scratch, scalars=1)
    qkv_reduce = Reduce(order, dp, d, (parts[:2], bits[0], None), (parts[2:], bits[1], None))
    body = functools.partial(down_kernel, [(0, 0), (1, 0), (0, half), (1, half)])
    fourth = [arr((size // 4, width))] * 4
    ffn2, *send = order("down", body, [arr(token), *fourth], (act_a, act_b, w_down))
    up_sum, down_sum = up_reduce.stage()
    send = [pair_gather(order.then(x)) for x in send]
    order.wait(*send, dn1_core)
    (ffn_chip,) = order("add", add_pair_kernel, [arr(token)], (t_arg, ffn2, *send), scalars=1)
    ffn_chip = to_chip(ffn_chip)
    qkv_reduce.stage()
    blocks = quarters("wwwwabrw", *token)
    args = (dn1_own, dn1_core, dn1_chip, x, dresid_a, dresid_b, gain1)
    (x_grad,) = order("last", last_kernel, [arr(token, F32)], args, blocks=blocks)
    qkv_reduce.stage()
    body = functools.partial(down_kernel, [(0, i * half) for i in range(4)])
    ffn0, *send = order("down", body, [arr(token), *fourth], (act_near, w_down))
    send = [pair_gather(x) for x in send]
    order.wait(*send)
    (ffn0,) = order("add", add_pair_kernel, [arr(token)], (t_arg, ffn0, *send), scalars=1)
    args = (resid, ffn0, ffn_chip, seg, down_bias[None])
    (output,) = order("result", result_kernel, [arr(token)], args, blocks=quarters("wwwsrw", *token))
    chunk = width // dp // 4
    if low:
        first, second = qkv_reduce.stage()
        lines = qkv_reduce.rest(first[tile : tile + 6, :tile].T, False)
        both = jnp.concatenate([qkv_reduce.rest(p[:tile], False) for p in (first, second)], 1)
        qkv_sum = both[:, : 3 * local_width].reshape(width // dp, 3, local_width).transpose(1, 0, 2)
        out_own, out_send = both[:, 3 * local_width : 4 * local_width], both[:, 4 * local_width :]
    else:
        square = (tile, local_width)
        outs = [arr((3, *square), F32), arr(square, F32), arr(square), arr((tile, 8), F32)]
        args = (*qkv_reduce.own, *qkv_reduce.got)
        qkv_sum, out_own, out_send, lines = order("finish", finish_kernel, outs, args)
    out_sum = out_own + to_chip(out_send)
    lines = jnp.sum(lax.all_gather(lines, "tensor", axis=0), 0)
    vectors = lax.dynamic_slice_in_dim(lines, t * chunk, chunk, 0)
    return (output[None], x_grad[None], qkv_sum, out_sum.T, up_sum, down_sum, *(vectors[:, i] for i in range(6)))


def solution(mesh):
    row = P("dp", "tensor", None)
    matrix = (P(None, None, "tensor"), P("tensor", None), P(None, "tensor"), P("tensor", None))
    in_specs = (row, P("dp", "tensor"), *matrix) + (P(),) * 6 + (row,)
    vector = P(("dp", "tensor"))
    out_specs = (row, row, P(None, "dp", "tensor"), P("tensor", "dp"), P("dp", "tensor"), P("tensor", "dp")) + (vector,) * 6
    run = functools.partial(local, mesh.shape["dp"])
    return jax.shard_map(run, mesh=mesh, in_specs=in_specs, out_specs=out_specs, check_vma=False)
```
